512 devices in a mesh: gx: 128 (over z, x, y_hi), gy: 4 (over y_lo, core).
Axes of the slice: x: 4, y: 4 (y_hi: 2, y_lo: 2; y = y_hi * 2 + y_lo), z: 16, core: 2. Of those that a mesh axis runs over, the one named last changes fastest.
Arguments:
- populations: float32 [19, 256, 64, 256], P(None, 'gx', 'gy'), may hold values from 0.01 to 0.15
- target_density: float32 [256, 64, 256], P('gx', 'gy'), may hold values from 1.1 to 1.9
- weight_in: float32 [19, 32], replicated, may hold values from -1.25 to 1.25
- bias_in: float32 [32], replicated, may hold values from -3 to 3
- weight_out: float32 [32, 19], replicated, may hold values from -1 to 1
- bias_out: float32 [19], replicated, may hold values from -4 to 4
Outputs:
- moments: float32 [4, 256, 64, 256], P(None, 'gx', 'gy')
- grad_weight_in: float32 [19, 32], replicated
- grad_bias_in: float32 [32], replicated
- grad_weight_out: float32 [32, 19], replicated
- grad_bias_out: float32 [19], replicated
The draws below stay inside these ranges and needn't reach their ends.
All inputs are finite; a program needn't handle non-finite values.
Results may differ from the reference program's by a relative error of at most 0.0003.
Values sent between devices are 32-bit elements; how exact they have to be, the bound alone decides.
No kernel may reach another device: no remote copies, remote signals or barrier semaphores. Data moves between devices by JAX's collectives and lax.ppermute only.
A program may use at most 64 MiB of HBM per device.

```python
import math
import jax
import jax.numpy as jnp
from jax import lax

VELOCITIES = 19
HIDDEN_UNITS = 32
NX = 256
NY = 64
NZ = 256


def levels(rng, dims, shards, low, largest):
    loudness = 1.0
    for position, shards_of in shards:
        steps = jax.random.uniform(jax.random.fold_in(jax.random.fold_in(rng, 6), position), (shards_of,), jnp.float32, low / len(shards), largest / len(shards))
        loudness = loudness * jnp.repeat(jnp.exp(steps), dims[position] // shards_of).reshape((-1,) + (1,) * (len(dims) - 1 - position))
    return loudness


def normal_values(key, dims, deviation, limit, kind=jnp.bfloat16):
    entries = jax.random.normal(key, dims, jnp.float32) * deviation
    return jnp.minimum(jnp.maximum(entries, -limit), limit).astype(kind)


def setup_inputs(seed: int = 0) -> dict:
    key_of = jax.random.split(jax.random.key(seed), 7)
    populations = jnp.clip(0.01 + 0.14 * jax.random.uniform(key_of[0], (VELOCITIES, NX, NY, NZ), jnp.float32) ** levels(key_of[0], (VELOCITIES, NX, NY, NZ), ((1, 128), (2, 4)), -0.2, 0.2), 0.01, 0.15)
    target_density = jnp.clip(1.1 + 0.79999995 * jax.random.uniform(key_of[1], (NX, NY, NZ), jnp.float32) ** levels(key_of[1], (NX, NY, NZ), ((0, 128), (1, 4)), -0.2, 0.2), 1.1, 1.9)
    weight_in = normal_values(key_of[2], (VELOCITIES, HIDDEN_UNITS), VELOCITIES ** -0.5, 1.25, jnp.float32)
    bias_in = normal_values(key_of[3], (HIDDEN_UNITS,), 0.5, 3.0, jnp.float32)
    weight_out = normal_values(key_of[4], (HIDDEN_UNITS, VELOCITIES), HIDDEN_UNITS ** -0.5, 1.0, jnp.float32)
    bias_out = normal_values(key_of[5], (VELOCITIES,), 1.0, 4.0, jnp.float32)
    return {"populations": populations, "target_density": target_density, "weight_in": weight_in, "bias_in": bias_in, "weight_out": weight_out, "bias_out": bias_out}


velocity_table = ((0, 0, 0), (1, 0, 0), (-1, 0, 0), (0, 1, 0), (0, -1, 0), (0, 0, 1), (0, 0, -1), (1, 1, 0), (-1, -1, 0), (1, -1, 0), (-1, 1, 0), (1, 0, 1), (-1, 0, -1), (1, 0, -1), (-1, 0, 1), (0, 1, 1), (0, -1, -1), (0, 1, -1), (0, -1, 1))
lattice_weights = (1.0 / 3.0,) + (1.0 / 18.0,) * 6 + (1.0 / 36.0,) * 12
input_scale = 8.0
output_scale = 0.05
relax_time = 0.8

def collide(lattice, weight_in, bias_in, weight_out, bias_out):
    highest = lax.Precision.HIGHEST
    vel_table = jnp.array(velocity_table, jnp.float32)
    lattice_w = jnp.array(lattice_weights, jnp.float32)
    bcast_shape = (19,) + (1,) * (lattice.ndim - 1)
    density = lax.optimization_barrier(jnp.sum(lattice, axis=0))
    momentum = jnp.einsum('qd,q...->d...', vel_table, lattice, precision=highest)
    projected = jnp.einsum('qd,d...->q...', vel_table, momentum, precision=highest)
    speed_sq = lax.optimization_barrier(jnp.sum(momentum * momentum, axis=0))
    equilibrium = lattice_w.reshape(bcast_shape) * (density + 3.0 * projected + 4.5 * projected * projected - 1.5 * speed_sq)
    excess = lattice - equilibrium
    hidden = jnp.tanh(jnp.einsum('qh,q...->h...', weight_in, input_scale * excess, precision=highest) + bias_in.reshape((-1,) + (1,) * (lattice.ndim - 1)))
    correction = output_scale * (jnp.einsum('hq,h...->q...', weight_out, hidden, precision=highest) + bias_out.reshape(bcast_shape))
    return lattice - excess / relax_time + correction

def stream(lattice, heading):
    return jnp.stack([jnp.roll(lattice[q], tuple((heading * c for c in velocity_table[q])), axis=(0, 1, 2)) for q in range(19)])

def moments_of(lattice):
    vel_table = jnp.array(velocity_table, jnp.float32)
    density = lax.optimization_barrier(jnp.sum(lattice, axis=0))
    momentum = jnp.einsum('qd,q...->d...', vel_table, lattice, precision=lax.Precision.HIGHEST)
    return jnp.concatenate([density[None], momentum], axis=0)

def slab_collide(lattice, params):

    def advance(slab_at):
        return collide(lax.dynamic_index_in_dim(lattice, slab_at, 1, False), *params)
    stacked = lax.map(advance, jnp.arange(lattice.shape[1], dtype=jnp.int32))
    return jnp.moveaxis(stacked, 0, 1)

def slab_pullback(lattice, cotangent, params):

    def advance(running, slab_at):
        sheet_now = lax.dynamic_index_in_dim(lattice, slab_at, 1, False)
        upstream = lax.dynamic_index_in_dim(cotangent, slab_at, 1, False)
        _, pullback = jax.vjp(collide, sheet_now, *params)
        gradients = pullback(upstream)
        return (tuple((a + b for a, b in zip(running, gradients[1:]))), gradients[0])
    initial = tuple((jnp.zeros(p.shape, jnp.float32) for p in params))
    summed, sheets = lax.scan(advance, initial, jnp.arange(lattice.shape[1], dtype=jnp.int32))
    return (jnp.moveaxis(sheets, 0, 1), summed)

def reference(populations, target_density, weight_in, bias_in, weight_out, bias_out):
    params = (weight_in, bias_in, weight_out, bias_out)
    after1 = stream(slab_collide(populations, params), 1)
    after2 = stream(slab_collide(after1, params), 1)
    moments = moments_of(after2)
    residual_scale = 1.0 / math.sqrt(NX * NY * NZ)
    grad_density = (moments[0] - target_density) * residual_scale
    cotangent = jnp.broadcast_to(grad_density[None], after2.shape)
    back1 = stream(cotangent, -1)
    g_after1, late = slab_pullback(after1, back1, params)
    back0 = stream(g_after1, -1)
    _, early = slab_pullback(populations, back0, params)
    return (moments, early[0] + late[0], early[1] + late[1], early[2] + late[2], early[3] + late[3])
```

```python
import math

import jax
import jax.numpy as jnp
from jax import lax
from jax.experimental import pallas as pl
from jax.experimental.pallas import tpu as pltpu
from jax.sharding import Mesh, PartitionSpec as P

velocity_table = (
    (0, 0, 0),
    (1, 0, 0),
    (-1, 0, 0),
    (0, 1, 0),
    (0, -1, 0),
    (0, 0, 1),
    (0, 0, -1),
    (1, 1, 0),
    (-1, -1, 0),
    (1, -1, 0),
    (-1, 1, 0),
    (1, 0, 1),
    (-1, 0, -1),
    (1, 0, -1),
    (-1, 0, 1),
    (0, 1, 1),
    (0, -1, -1),
    (0, 1, -1),
    (0, -1, 1),
)
lattice_weights = (1.0 / 3.0,) + (1.0 / 18.0,) * 6 + (1.0 / 36.0,) * 12
input_scale = 8.0
output_scale = 0.05
relax_time = 0.8

Q = 19
H = 32
NZ = 256
YW = 20
ROWS = 6 * YW
G1 = ROWS // 8
B2 = 16
G2 = 11
MARGIN = 24
SP = 8
QS = 20 * SP
HS = H * SP
F32 = jnp.float32
BF16 = jnp.bfloat16


def row_shift(q):
    return YW * velocity_table[q][0] + velocity_table[q][1]


def split(x):
    hi = x.astype(BF16)
    lo = (x - hi.astype(F32)).astype(BF16)
    return hi, lo


def mm(a, b):
    return lax.dot_general(a, b, (((1,), (0,)), ((), ())), preferred_element_type=F32)


def mm_nt(a, b):
    return lax.dot_general(a, b, (((1,), (1,)), ((), ())), preferred_element_type=F32)


def prep_kernel(win_ref, bin_ref, wout_ref, lin_ref, lint_ref, lout_ref, loutt_ref):
    hp = lax.Precision.HIGHEST
    nt = (((1,), (1,)), ((), ()))
    eq = (
        lax.broadcasted_iota(jnp.int32, (QS, Q), 0) // SP
        == lax.broadcasted_iota(jnp.int32, (QS, Q), 1)
    ).astype(F32)
    eh = (
        lax.broadcasted_iota(jnp.int32, (HS, H), 0) // SP
        == lax.broadcasted_iota(jnp.int32, (HS, H), 1)
    ).astype(F32)
    rq = lax.broadcasted_iota(jnp.int32, (QS, HS), 0)
    rh = lax.broadcasted_iota(jnp.int32, (QS, HS), 1)
    mask_qh = (rq % SP) == (rh % SP)
    ch = lax.broadcasted_iota(jnp.int32, (HS, QS), 0)
    cq = lax.broadcasted_iota(jnp.int32, (HS, QS), 1)
    mask_hq = (ch % SP) == (cq % SP)

    t_in = lax.dot_general(eq, win_ref[...] * input_scale, (((1,), (0,)), ((), ())), precision=hp, preferred_element_type=F32)
    t_out = lax.dot_general(eq, wout_ref[...] * output_scale, nt, precision=hp, preferred_element_type=F32)
    is_bias = lax.broadcasted_iota(jnp.int32, (QS, H), 0) >= Q * SP
    t_inb = jnp.where(is_bias, jnp.broadcast_to(bin_ref[...], (QS, H)), t_in)

    def put(ref, a, b, mask):
        full = lax.dot_general(a, b, nt, precision=hp, preferred_element_type=F32)
        hi, lo = split(jnp.where(mask, full, 0.0))
        n = full.shape[1]
        ref[:, 0:n] = hi
        ref[:, n : 2 * n] = hi
        ref[:, 2 * n : 3 * n] = lo

    put(lin_ref, eh, t_inb, mask_hq)
    put(lint_ref, t_in, eh, mask_qh)
    put(lout_ref, t_out, eh, mask_qh)
    put(loutt_ref, eh, t_out, mask_hq)


def equilibrium_parts(f):
    density = f[0]
    for q in range(1, Q):
        density = density + f[q]
    momentum = []
    for a in range(3):
        plus = None
        minus = None
        for q in range(Q):
            c = velocity_table[q][a]
            if c == 1:
                plus = f[q] if plus is None else plus + f[q]
            elif c == -1:
                minus = f[q] if minus is None else minus + f[q]
        momentum.append(plus - minus)
    return density, momentum


def project(q, m):
    out = None
    for a in range(3):
        c = velocity_table[q][a]
        if c == 0:
            continue
        if out is None:
            out = m[a] if c == 1 else -m[a]
        else:
            out = out + m[a] if c == 1 else out - m[a]
    return out


def excess_of(f):
    density, m = equilibrium_parts(f)
    base = density - 1.5 * (m[0] * m[0] + m[1] * m[1] + m[2] * m[2])
    excess = [f[0] - lattice_weights[0] * base]
    for q in range(1, Q, 2):
        w = lattice_weights[q]
        cm = project(q, m)
        even = w * (base + 4.5 * (cm * cm))
        odd = (3.0 * w) * cm
        excess.append(f[q] - (even + odd))
        excess.append(f[q + 1] - (even - odd))
    return excess, m


def rows8(x, q):
    return x[q * SP : (q + 1) * SP, :]


def collide(f, lin_ref, lout_ref, bout_ref, save_x, save_h):
    excess, m = excess_of(f)
    x = jnp.concatenate(excess + [jnp.ones((SP, NZ), F32)], axis=0)
    xhi, xlo = split(x)
    save_x(xhi, xlo)
    pre = mm(lin_ref[...], jnp.concatenate([xhi, xlo, xhi], axis=0))
    hid = jnp.tanh(pre)
    hhi, hlo = split(hid)
    save_h(hhi, hlo)
    corr = mm(lout_ref[...], jnp.concatenate([hhi, hlo, hhi], axis=0))
    out = []
    for q in range(Q):
        out.append(f[q] - excess[q] * (1.0 / relax_time) + (rows8(corr, q) + output_scale * bout_ref[q]))
    return out, m


def zroll(x, step):
    if step == 0:
        return x
    return pltpu.roll(x, step % NZ, 1)


def main_kernel(
    parity_ref,
    bout_ref,
    own_ref,
    a_ref,
    b_ref,
    target_ref,
    lin_ref,
    lint_ref,
    lout_ref,
    loutt_ref,
    moments_ref,
    grads_ref,
    fs,
    c1s,
    c2s,
    g1s,
    rs,
    x1s,
    h1s,
    x2s,
    h2s,
    m2s,
    acc_in,
    acc_out,
    acc_b,
    sems,
):
    parity = parity_ref[0]
    a_row = pl.multiple_of(80 * (1 - parity), 8)
    b_row = pl.multiple_of(80 * parity, 8)
    copies = [
        pltpu.make_async_copy(own_ref, fs.at[:, 40:80, :], sems.at[0]),
        pltpu.make_async_copy(a_ref, fs.at[:, pl.ds(a_row, 40), :], sems.at[1]),
        pltpu.make_async_copy(b_ref, fs.at[:, pl.ds(b_row, 40), :], sems.at[2]),
    ]
    for c in copies:
        c.start()
    acc_in[...] = jnp.zeros_like(acc_in)
    acc_out[...] = jnp.zeros_like(acc_out)
    acc_b[...] = jnp.zeros_like(acc_b)
    rs[...] = jnp.zeros_like(rs)
    zero_top = jnp.zeros((Q, MARGIN, NZ), F32)
    c1s[:, 0:MARGIN, :] = zero_top
    c1s[:, MARGIN + ROWS :, :] = zero_top
    g1s[:, 0 : MARGIN + B2, :] = jnp.zeros((Q, MARGIN + B2, NZ), F32)
    g1s[:, MARGIN + B2 + 8 * G2 :, :] = jnp.zeros((Q, MARGIN + ROWS - B2 - 8 * G2, NZ), F32)
    for c in copies:
        c.wait()

    def load(ref, q, row, off):
        base = (off // 8) * 8
        rem = off % 8
        start = pl.multiple_of(row + base, 8)
        if rem == 0:
            return ref[q, pl.ds(start, 8), :]
        both = ref[q, pl.ds(start, 16), :]
        return both[rem : rem + 8, :]

    def stage1(g, _):
        row = pl.multiple_of(g * 8, 8)
        f = [fs[q, pl.ds(row, 8), :] for q in range(Q)]

        def save_x(hi, lo):
            x1s[g, 0:QS, :] = hi
            x1s[g, QS : 2 * QS, :] = lo

        def save_h(hi, lo):
            h1s[g, 0:HS, :] = hi
            h1s[g, HS : 2 * HS, :] = lo

        out, _m = collide(f, lin_ref, lout_ref, bout_ref, save_x, save_h)
        for q in range(Q):
            c1s[q, pl.ds(row + MARGIN, 8), :] = zroll(out[q], velocity_table[q][2])
        return 0

    lax.fori_loop(0, G1, stage1, 0)

    def stage2(g, _):
        row = pl.multiple_of(g * 8 + B2, 8)
        f = [load(c1s, q, row, MARGIN - row_shift(q)) for q in range(Q)]

        def save_x(hi, lo):
            x2s[g, 0:QS, :] = hi
            x2s[g, QS : 2 * QS, :] = lo

        def save_h(hi, lo):
            h2s[g, 0:HS, :] = hi
            h2s[g, HS : 2 * HS, :] = lo

        out, m = collide(f, lin_ref, lout_ref, bout_ref, save_x, save_h)
        for a in range(3):
            m2s[g, a] = m[a]
        for q in range(Q):
            c2s[q, pl.ds(row, 8), :] = zroll(out[q], velocity_table[q][2])
        return 0

    lax.fori_loop(0, G2, stage2, 0)

    residual_scale = 1.0 / math.sqrt(256 * 64 * 256)
    for x in range(2):
        for half in range(2):
            first = YW * (x + 2) + 2 + 8 * half
            f = [c2s[q, first - row_shift(q) : first - row_shift(q) + 8, :] for q in range(Q)]
            density, m = equilibrium_parts(f)
            moments_ref[0, x, 8 * half : 8 * half + 8, :] = density
            for a in range(3):
                moments_ref[a + 1, x, 8 * half : 8 * half + 8, :] = m[a]
            r = (density - target_ref[x, 8 * half : 8 * half + 8, :]) * residual_scale
            rs[0, MARGIN + first : MARGIN + first + 8, :] = r
            rs[1, MARGIN + first : MARGIN + first + 8, :] = zroll(r, -1)
            rs[2, MARGIN + first : MARGIN + first + 8, :] = zroll(r, 1)

    def pull_params(gq, x_hl, h_hl, g):
        gs = jnp.concatenate(gq + [jnp.zeros((SP, NZ), F32)], axis=0)
        ghi, glo = split(gs)
        dh = mm(loutt_ref[...], jnp.concatenate([ghi, glo, ghi], axis=0))
        hhi = h_hl[g, 0:HS, :]
        hlo = h_hl[g, HS : 2 * HS, :]
        hid = hhi.astype(F32) + hlo.astype(F32)
        dpre = dh * (1.0 - hid * hid)
        dhi, dlo = split(dpre)
        xhi = x_hl[g, 0:QS, :]
        xlo = x_hl[g, QS : 2 * QS, :]
        acc_in[...] += mm_nt(
            jnp.concatenate([xhi, xlo, xhi], axis=1), jnp.concatenate([dhi, dhi, dlo], axis=1)
        )
        acc_out[...] += mm_nt(
            jnp.concatenate([ghi, glo, ghi], axis=1), jnp.concatenate([hhi, hhi, hlo], axis=1)
        )
        acc_b[...] += gs
        return dhi, dlo

    def stage4(g, _):
        row = pl.multiple_of(g * 8 + B2, 8)
        gq = []
        for q in range(Q):
            cz = velocity_table[q][2]
            gq.append(load(rs, {0: 0, 1: 1, -1: 2}[cz], row, MARGIN + row_shift(q)))
        dhi, dlo = pull_params(gq, x2s, h2s, g)
        back = mm(lint_ref[...], jnp.concatenate([dhi, dlo, dhi], axis=0))
        m = [m2s[g, a] for a in range(3)]
        de = [rows8(back, q) - gq[q] * (1.0 / relax_time) for q in range(Q)]
        t = [lattice_weights[q] * de[q] for q in range(Q)]
        drho = t[0]
        for q in range(1, Q):
            drho = drho + t[q]
        u = [None] * Q
        for q in range(1, Q, 2):
            cm = 9.0 * project(q, m)
            u[q] = t[q] * (3.0 + cm)
            u[q + 1] = t[q + 1] * (3.0 - cm)
        dm = []
        for a in range(3):
            plus = None
            minus = None
            for q in range(Q):
                c = velocity_table[q][a]
                if c == 1:
                    plus = u[q] if plus is None else plus + u[q]
                elif c == -1:
                    minus = u[q] if minus is None else minus + u[q]
            dm.append(plus - minus - 3.0 * m[a] * drho)
        for q in range(Q):
            df = gq[q] + de[q] - drho
            if q:
                df = df - project(q, dm)
            g1s[q, pl.ds(row + MARGIN, 8), :] = zroll(df, -velocity_table[q][2])
        return 0

    lax.fori_loop(0, G2, stage4, 0)

    def stage5(g, _):
        row = pl.multiple_of(g * 8, 8)
        gq = [load(g1s, q, row, MARGIN + row_shift(q)) for q in range(Q)]
        pull_params(gq, x1s, h1s, g)
        return 0

    lax.fori_loop(0, G1, stage5, 0)

    hp = lax.Precision.HIGHEST
    rq = lax.broadcasted_iota(jnp.int32, (QS, HS), 0)
    rh = lax.broadcasted_iota(jnp.int32, (QS, HS), 1)
    mask = (rq % SP) == (rh % SP)
    fold = (
        lax.broadcasted_iota(jnp.int32, (HS, H), 0) // SP
        == lax.broadcasted_iota(jnp.int32, (HS, H), 1)
    ).astype(F32)

    def trace(acc):
        kept = jnp.where(mask, acc[...], 0.0).reshape(20, SP, HS).sum(axis=1)
        return lax.dot_general(
            kept, fold, (((1,), (0,)), ((), ())), precision=hp, preferred_element_type=F32
        )

    q_index = lax.broadcasted_iota(jnp.int32, (20, H), 0)
    d_in = trace(acc_in) * jnp.where(q_index < Q, input_scale, 1.0)
    d_out = trace(acc_out) * output_scale
    d_b = acc_b[...].reshape(20, SP, NZ).sum(axis=1).sum(axis=1, keepdims=True) * output_scale
    grads_ref[...] = jnp.zeros_like(grads_ref)
    grads_ref[0:10, 0:H] = d_in[0:10]
    grads_ref[0:10, H : 2 * H] = d_in[10:20]
    grads_ref[0:10, 2 * H : 3 * H] = d_out[0:10]
    grads_ref[0:10, 3 * H : 4 * H] = d_out[10:20]
    for i in range(4):
        grads_ref[10:15, i : i + 1] = d_b[5 * i : 5 * i + 5]


def unpack(grads):
    d_in = jnp.concatenate([grads[0:10, 0:H], grads[0:10, H : 2 * H]], axis=0)
    d_out = jnp.concatenate([grads[0:10, 2 * H : 3 * H], grads[0:10, 3 * H :]], axis=0)
    d_b = grads[10:15, 0:4].T.reshape(20)
    return d_in[0:Q], d_in[Q], d_out[0:Q].T, d_b[0:Q]


def prep(weight_in, bias_in, weight_out):
    return pl.pallas_call(
        prep_kernel,
        out_shape=(
            jax.ShapeDtypeStruct((HS, 3 * QS), BF16),
            jax.ShapeDtypeStruct((QS, 3 * HS), BF16),
            jax.ShapeDtypeStruct((QS, 3 * HS), BF16),
            jax.ShapeDtypeStruct((HS, 3 * QS), BF16),
        ),
        compiler_params=pltpu.CompilerParams(vmem_limit_bytes=24 * 1024 * 1024),
        name="prep",
    )(weight_in, bias_in.reshape(1, H), weight_out)


def main(parity, bias_out, own, a, b, target, mats):
    vmem = pl.BlockSpec(memory_space=pltpu.VMEM)
    smem = pl.BlockSpec(memory_space=pltpu.SMEM)
    anym = pl.BlockSpec(memory_space=pl.ANY)
    span = 2 * MARGIN + ROWS
    return pl.pallas_call(
        main_kernel,
        out_shape=(
            jax.ShapeDtypeStruct((4, 2, 16, NZ), F32),
            jax.ShapeDtypeStruct((16, 128), F32),
        ),
        in_specs=[smem, smem, anym, anym, anym, vmem, vmem, vmem, vmem, vmem],
        out_specs=(vmem, vmem),
        scratch_shapes=[
            pltpu.VMEM((Q, ROWS, NZ), F32),
            pltpu.VMEM((Q, span, NZ), F32),
            pltpu.VMEM((Q, ROWS, NZ), F32),
            pltpu.VMEM((Q, span, NZ), F32),
            pltpu.VMEM((3, span, NZ), F32),
            pltpu.VMEM((G1, 2 * QS, NZ), BF16),
            pltpu.VMEM((G1, 2 * HS, NZ), BF16),
            pltpu.VMEM((G2, 2 * QS, NZ), BF16),
            pltpu.VMEM((G2, 2 * HS, NZ), BF16),
            pltpu.VMEM((G2, 3, SP, NZ), F32),
            pltpu.VMEM((QS, HS), F32),
            pltpu.VMEM((QS, HS), F32),
            pltpu.VMEM((QS, NZ), F32),
            pltpu.SemaphoreType.DMA((3,)),
        ],
        compiler_params=pltpu.CompilerParams(vmem_limit_bytes=48 * 1024 * 1024),
        name="lattice",
    )(parity, bias_out, own, a, b, target, *mats)


def body(populations, target_density, weight_in, bias_in, weight_out, bias_out):
    gx, gy = ("zh", "zl", "x", "yh"), ("yl", "c")
    nx, ny = lax.axis_size(gx), lax.axis_size(gy)
    mats = prep(weight_in, bias_in, weight_out)
    last = populations[:, :, 14:16, :].reshape(Q, 4, NZ)
    first = populations[:, :, 0:2, :].reshape(Q, 4, NZ)
    before = lax.ppermute(last, gy, [(j, (j + 1) % ny) for j in range(ny)])
    after = lax.ppermute(first, gy, [((j + 1) % ny, j) for j in range(ny)])
    own = jnp.concatenate(
        [
            before[:, 0:2],
            populations[:, 0],
            after[:, 0:2],
            before[:, 2:4],
            populations[:, 1],
            after[:, 2:4],
        ],
        axis=1,
    )
    pair = [(i, i ^ 1) for i in range(nx)]
    cross = [(i, (i + 1) % nx if i % 2 else (i - 1) % nx) for i in range(nx)]
    b = lax.ppermute(own, gx, cross)
    a = lax.ppermute(own, gx, pair)
    parity = (lax.axis_index("yh") % 2).astype(jnp.int32).reshape(1)
    moments, grads = main(parity, bias_out, own, a, b, target_density, mats)
    grads = lax.psum(grads, ("yl", "c"))
    grads = lax.psum(grads, "yh")
    grads = lax.psum(grads, "x")
    grads = lax.psum(grads, "zl")
    grads = lax.psum(grads, "zh")
    return (moments, *unpack(grads))


def solution(mesh):
    fine = Mesh(mesh.devices.reshape(4, 4, 4, 2, 2, 2), ("zh", "zl", "x", "yh", "yl", "c"))
    gx, gy = ("zh", "zl", "x", "yh"), ("yl", "c")
    placed = (P(None, gx, gy, None), P(gx, gy, None), P(), P(), P(), P())
    return jax.shard_map(
        body,
        mesh=fine,
        in_specs=placed,
        out_specs=(P(None, gx, gy, None), P(), P(), P(), P()),
        check_vma=False,
    )
```

```python
import math

import jax
import jax.numpy as jnp
from jax import lax
from jax.experimental import pallas as pl
from jax.experimental.pallas import tpu as pltpu
from jax.sharding import Mesh, PartitionSpec as P

velocity_table = (
    (0, 0, 0),
    (1, 0, 0),
    (-1, 0, 0),
    (0, 1, 0),
    (0, -1, 0),
    (0, 0, 1),
    (0, 0, -1),
    (1, 1, 0),
    (-1, -1, 0),
    (1, -1, 0),
    (-1, 1, 0),
    (1, 0, 1),
    (-1, 0, -1),
    (1, 0, -1),
    (-1, 0, 1),
    (0, 1, 1),
    (0, -1, -1),
    (0, 1, -1),
    (0, -1, 1),
)
lattice_weights = (1.0 / 3.0,) + (1.0 / 18.0,) * 6 + (1.0 / 36.0,) * 12
input_scale = 8.0
output_scale = 0.05
relax_time = 0.8

Q = 19
H = 32
NZ = 256
YW = 20
ROWS = 6 * YW
G1 = ROWS // 8
B2 = 16
G2 = 11
MARGIN = 24
SP = 8
QS = 20 * SP
HS = H * SP
F32 = jnp.float32
BF16 = jnp.bfloat16


def row_shift(q):
    return YW * velocity_table[q][0] + velocity_table[q][1]


def split(x):
    hi = x.astype(BF16)
    lo = (x - hi.astype(F32)).astype(BF16)
    return hi, lo


def mm(a, b):
    return lax.dot_general(a, b, (((1,), (0,)), ((), ())), preferred_element_type=F32)


def mm_nt(a, b):
    return lax.dot_general(a, b, (((1,), (1,)), ((), ())), preferred_element_type=F32)


def prep_kernel(win_ref, bin_ref, wout_ref, lin_ref, lint_ref, lout_ref, loutt_ref):
    hp = lax.Precision.HIGHEST
    nt = (((1,), (1,)), ((), ()))
    eq = (
        lax.broadcasted_iota(jnp.int32, (QS, Q), 0) // SP
        == lax.broadcasted_iota(jnp.int32, (QS, Q), 1)
    ).astype(F32)
    eh = (
        lax.broadcasted_iota(jnp.int32, (HS, H), 0) // SP
        == lax.broadcasted_iota(jnp.int32, (HS, H), 1)
    ).astype(F32)
    rq = lax.broadcasted_iota(jnp.int32, (QS, HS), 0)
    rh = lax.broadcasted_iota(jnp.int32, (QS, HS), 1)
    mask_qh = (rq % SP) == (rh % SP)
    ch = lax.broadcasted_iota(jnp.int32, (HS, QS), 0)
    cq = lax.broadcasted_iota(jnp.int32, (HS, QS), 1)
    mask_hq = (ch % SP) == (cq % SP)

    t_in = lax.dot_general(eq, win_ref[...] * input_scale, (((1,), (0,)), ((), ())), precision=hp, preferred_element_type=F32)
    t_out = lax.dot_general(eq, wout_ref[...] * output_scale, nt, precision=hp, preferred_element_type=F32)
    is_bias = lax.broadcasted_iota(jnp.int32, (QS, H), 0) >= Q * SP
    t_inb = jnp.where(is_bias, jnp.broadcast_to(bin_ref[...], (QS, H)), t_in)

    def put(ref, a, b, mask):
        full = lax.dot_general(a, b, nt, precision=hp, preferred_element_type=F32)
        hi, lo = split(jnp.where(mask, full, 0.0))
        n = full.shape[1]
        ref[:, 0:n] = hi
        ref[:, n : 2 * n] = hi
        ref[:, 2 * n : 3 * n] = lo

    put(lin_ref, eh, t_inb, mask_hq)
    put(lint_ref, t_in, eh, mask_qh)
    put(lout_ref, t_out, eh, mask_qh)
    put(loutt_ref, eh, t_out, mask_hq)


def equilibrium_parts(f):
    density = f[0]
    for q in range(1, Q):
        density = density + f[q]
    momentum = []
    for a in range(3):
        plus = None
        minus = None
        for q in range(Q):
            c = velocity_table[q][a]
            if c == 1:
                plus = f[q] if plus is None else plus + f[q]
            elif c == -1:
                minus = f[q] if minus is None else minus + f[q]
        momentum.append(plus - minus)
    return density, momentum


def project(q, m):
    out = None
    for a in range(3):
        c = velocity_table[q][a]
        if c == 0:
            continue
        if out is None:
            out = m[a] if c == 1 else -m[a]
        else:
            out = out + m[a] if c == 1 else out - m[a]
    return out


def excess_of(f):
    density, m = equilibrium_parts(f)
    base = density - 1.5 * (m[0] * m[0] + m[1] * m[1] + m[2] * m[2])
    excess = [f[0] - lattice_weights[0] * base]
    for q in range(1, Q, 2):
        w = lattice_weights[q]
        cm = project(q, m)
        even = w * (base + 4.5 * (cm * cm))
        odd = (3.0 * w) * cm
        excess.append(f[q] - (even + odd))
        excess.append(f[q + 1] - (even - odd))
    return excess, m


def rows8(x, q):
    return x[q * SP : (q + 1) * SP, :]


def collide(f, lin_ref, lout_ref, bout_ref, save_x, save_h):
    excess, m = excess_of(f)
    x = jnp.concatenate(excess + [jnp.ones((SP, NZ), F32)], axis=0)
    xhi, xlo = split(x)
    save_x(xhi, xlo)
    pre = mm(lin_ref[...], jnp.concatenate([xhi, xlo, xhi], axis=0))
    hid = jnp.tanh(pre)
    hhi, hlo = split(hid)
    save_h(hhi, hlo)
    corr = mm(lout_ref[...], jnp.concatenate([hhi, hlo, hhi], axis=0))
    out = []
    for q in range(Q):
        out.append(f[q] - excess[q] * (1.0 / relax_time) + (rows8(corr, q) + output_scale * bout_ref[q]))
    return out, m


def zroll(x, step):
    if step == 0:
        return x
    return pltpu.roll(x, step % NZ, 1)


def main_kernel(
    parity_ref,
    bout_ref,
    own_ref,
    b_ref,
    a_ref,
    target_ref,
    lin_ref,
    lint_ref,
    lout_ref,
    loutt_ref,
    moments_ref,
    grads_ref,
    fs,
    c1s,
    c2s,
    g1s,
    rs,
    x1s,
    h1s,
    x2s,
    h2s,
    m2s,
    acc_in,
    acc_out,
    acc_b,
    sems,
):
    parity = parity_ref[0]
    a_row = pl.multiple_of(80 * (1 - parity), 8)
    b_row = pl.multiple_of(80 * parity, 8)
    copies = [
        pltpu.make_async_copy(own_ref, fs.at[:, 40:80, :], sems.at[0]),
        pltpu.make_async_copy(a_ref, fs.at[:, pl.ds(a_row, 40), :], sems.at[1]),
        pltpu.make_async_copy(b_ref, fs.at[:, pl.ds(b_row, 40), :], sems.at[2]),
    ]
    for c in copies:
        c.start()
    acc_in[...] = jnp.zeros_like(acc_in)
    acc_out[...] = jnp.zeros_like(acc_out)
    acc_b[...] = jnp.zeros_like(acc_b)
    rs[...] = jnp.zeros_like(rs)
    zero_top = jnp.zeros((Q, MARGIN, NZ), F32)
    c1s[:, 0:MARGIN, :] = zero_top
    c1s[:, MARGIN + ROWS :, :] = zero_top
    g1s[:, 0 : MARGIN + B2, :] = jnp.zeros((Q, MARGIN + B2, NZ), F32)
    g1s[:, MARGIN + B2 + 8 * G2 :, :] = jnp.zeros((Q, MARGIN + ROWS - B2 - 8 * G2, NZ), F32)
    for c in copies:
        c.wait()

    def load(ref, q, row, off):
        base = (off // 8) * 8
        rem = off % 8
        start = pl.multiple_of(row + base, 8)
        if rem == 0:
            return ref[q, pl.ds(start, 8), :]
        both = ref[q, pl.ds(start, 16), :]
        return both[rem : rem + 8, :]

    def stage1(g, _):
        row = pl.multiple_of(g * 8, 8)
        f = [fs[q, pl.ds(row, 8), :] for q in range(Q)]

        def save_x(hi, lo):
            x1s[g, 0:QS, :] = hi
            x1s[g, QS : 2 * QS, :] = lo

        def save_h(hi, lo):
            h1s[g, 0:HS, :] = hi
            h1s[g, HS : 2 * HS, :] = lo

        out, _m = collide(f, lin_ref, lout_ref, bout_ref, save_x, save_h)
        for q in range(Q):
            c1s[q, pl.ds(row + MARGIN, 8), :] = zroll(out[q], velocity_table[q][2])
        return 0

    lax.fori_loop(0, G1, stage1, 0, unroll=True)

    def stage2(g, _):
        row = pl.multiple_of(g * 8 + B2, 8)
        f = [load(c1s, q, row, MARGIN - row_shift(q)) for q in range(Q)]

        def save_x(hi, lo):
            x2s[g, 0:QS, :] = hi
            x2s[g, QS : 2 * QS, :] = lo

        def save_h(hi, lo):
            h2s[g, 0:HS, :] = hi
            h2s[g, HS : 2 * HS, :] = lo

        out, m = collide(f, lin_ref, lout_ref, bout_ref, save_x, save_h)
        for a in range(3):
            m2s[g, a] = m[a]
        for q in range(Q):
            c2s[q, pl.ds(row, 8), :] = zroll(out[q], velocity_table[q][2])
        return 0

    lax.fori_loop(0, G2, stage2, 0, unroll=True)

    residual_scale = 1.0 / math.sqrt(256 * 64 * 256)
    for x in range(2):
        for half in range(2):
            first = YW * (x + 2) + 2 + 8 * half
            f = [c2s[q, first - row_shift(q) : first - row_shift(q) + 8, :] for q in range(Q)]
            density, m = equilibrium_parts(f)
            moments_ref[0, x, 8 * half : 8 * half + 8, :] = density
            for a in range(3):
                moments_ref[a + 1, x, 8 * half : 8 * half + 8, :] = m[a]
            r = (density - target_ref[x, 8 * half : 8 * half + 8, :]) * residual_scale
            rs[0, MARGIN + first : MARGIN + first + 8, :] = r
            rs[1, MARGIN + first : MARGIN + first + 8, :] = zroll(r, -1)
            rs[2, MARGIN + first : MARGIN + first + 8, :] = zroll(r, 1)

    def pull_params(gq, x_hl, h_hl, g):
        gs = jnp.concatenate(gq + [jnp.zeros((SP, NZ), F32)], axis=0)
        ghi, glo = split(gs)
        dh = mm(loutt_ref[...], jnp.concatenate([ghi, glo, ghi], axis=0))
        hhi = h_hl[g, 0:HS, :]
        hlo = h_hl[g, HS : 2 * HS, :]
        hid = hhi.astype(F32) + hlo.astype(F32)
        dpre = dh * (1.0 - hid * hid)
        dhi, dlo = split(dpre)
        xhi = x_hl[g, 0:QS, :]
        xlo = x_hl[g, QS : 2 * QS, :]
        acc_in[...] += mm_nt(
            jnp.concatenate([xhi, xlo, xhi], axis=1), jnp.concatenate([dhi, dhi, dlo], axis=1)
        )
        acc_out[...] += mm_nt(
            jnp.concatenate([ghi, glo, ghi], axis=1), jnp.concatenate([hhi, hhi, hlo], axis=1)
        )
        acc_b[...] += gs
        return dhi, dlo

    def stage4(g, _):
        row = pl.multiple_of(g * 8 + B2, 8)
        gq = []
        for q in range(Q):
            cz = velocity_table[q][2]
            gq.append(load(rs, {0: 0, 1: 1, -1: 2}[cz], row, MARGIN + row_shift(q)))
        dhi, dlo = pull_params(gq, x2s, h2s, g)
        back = mm(lint_ref[...], jnp.concatenate([dhi, dlo, dhi], axis=0))
        m = [m2s[g, a] for a in range(3)]
        de = [rows8(back, q) - gq[q] * (1.0 / relax_time) for q in range(Q)]
        t = [lattice_weights[q] * de[q] for q in range(Q)]
        drho = t[0]
        for q in range(1, Q):
            drho = drho + t[q]
        u = [None] * Q
        for q in range(1, Q, 2):
            cm = 9.0 * project(q, m)
            u[q] = t[q] * (3.0 + cm)
            u[q + 1] = t[q + 1] * (3.0 - cm)
        dm = []
        for a in range(3):
            plus = None
            minus = None
            for q in range(Q):
                c = velocity_table[q][a]
                if c == 1:
                    plus = u[q] if plus is None else plus + u[q]
                elif c == -1:
                    minus = u[q] if minus is None else minus + u[q]
            dm.append(plus - minus - 3.0 * m[a] * drho)
        for q in range(Q):
            df = gq[q] + de[q] - drho
            if q:
                df = df - project(q, dm)
            g1s[q, pl.ds(row + MARGIN, 8), :] = zroll(df, -velocity_table[q][2])
        return 0

    lax.fori_loop(0, G2, stage4, 0, unroll=True)

    def stage5(g, _):
        row = pl.multiple_of(g * 8, 8)
        gq = [load(g1s, q, row, MARGIN + row_shift(q)) for q in range(Q)]
        pull_params(gq, x1s, h1s, g)
        return 0

    lax.fori_loop(0, G1, stage5, 0, unroll=True)

    hp = lax.Precision.HIGHEST
    rq = lax.broadcasted_iota(jnp.int32, (QS, HS), 0)
    rh = lax.broadcasted_iota(jnp.int32, (QS, HS), 1)
    mask = (rq % SP) == (rh % SP)
    fold = (
        lax.broadcasted_iota(jnp.int32, (HS, H), 0) // SP
        == lax.broadcasted_iota(jnp.int32, (HS, H), 1)
    ).astype(F32)

    def trace(acc):
        kept = jnp.where(mask, acc[...], 0.0).reshape(20, SP, HS).sum(axis=1)
        return lax.dot_general(
            kept, fold, (((1,), (0,)), ((), ())), precision=hp, preferred_element_type=F32
        )

    q_index = lax.broadcasted_iota(jnp.int32, (20, H), 0)
    d_in = trace(acc_in) * jnp.where(q_index < Q, input_scale, 1.0)
    d_out = trace(acc_out) * output_scale
    d_b = acc_b[...].reshape(20, SP, NZ).sum(axis=1).sum(axis=1, keepdims=True) * output_scale
    grads_ref[...] = jnp.zeros_like(grads_ref)
    grads_ref[0:10, 0:H] = d_in[0:10]
    grads_ref[0:10, H : 2 * H] = d_in[10:20]
    grads_ref[0:10, 2 * H : 3 * H] = d_out[0:10]
    grads_ref[0:10, 3 * H : 4 * H] = d_out[10:20]
    for i in range(4):
        grads_ref[10:15, i : i + 1] = d_b[5 * i : 5 * i + 5]


def unpack(grads):
    d_in = jnp.concatenate([grads[0:10, 0:H], grads[0:10, H : 2 * H]], axis=0)
    d_out = jnp.concatenate([grads[0:10, 2 * H : 3 * H], grads[0:10, 3 * H :]], axis=0)
    d_b = grads[10:15, 0:4].T.reshape(20)
    return d_in[0:Q], d_in[Q], d_out[0:Q].T, d_b[0:Q]


def prep(weight_in, bias_in, weight_out):
    return pl.pallas_call(
        prep_kernel,
        out_shape=(
            jax.ShapeDtypeStruct((HS, 3 * QS), BF16),
            jax.ShapeDtypeStruct((QS, 3 * HS), BF16),
            jax.ShapeDtypeStruct((QS, 3 * HS), BF16),
            jax.ShapeDtypeStruct((HS, 3 * QS), BF16),
        ),
        compiler_params=pltpu.CompilerParams(vmem_limit_bytes=24 * 1024 * 1024),
        name="prep",
    )(weight_in, bias_in.reshape(1, H), weight_out)


def main(parity, bias_out, own, a, b, target, mats):
    vmem = pl.BlockSpec(memory_space=pltpu.VMEM)
    smem = pl.BlockSpec(memory_space=pltpu.SMEM)
    anym = pl.BlockSpec(memory_space=pl.ANY)
    span = 2 * MARGIN + ROWS
    return pl.pallas_call(
        main_kernel,
        out_shape=(
            jax.ShapeDtypeStruct((4, 2, 16, NZ), F32),
            jax.ShapeDtypeStruct((16, 128), F32),
        ),
        in_specs=[smem, smem, anym, anym, anym, vmem, vmem, vmem, vmem, vmem],
        out_specs=(vmem, vmem),
        scratch_shapes=[
            pltpu.VMEM((Q, ROWS, NZ), F32),
            pltpu.VMEM((Q, span, NZ), F32),
            pltpu.VMEM((Q, ROWS, NZ), F32),
            pltpu.VMEM((Q, span, NZ), F32),
            pltpu.VMEM((3, span, NZ), F32),
            pltpu.VMEM((G1, 2 * QS, NZ), BF16),
            pltpu.VMEM((G1, 2 * HS, NZ), BF16),
            pltpu.VMEM((G2, 2 * QS, NZ), BF16),
            pltpu.VMEM((G2, 2 * HS, NZ), BF16),
            pltpu.VMEM((G2, 3, SP, NZ), F32),
            pltpu.VMEM((QS, HS), F32),
            pltpu.VMEM((QS, HS), F32),
            pltpu.VMEM((QS, NZ), F32),
            pltpu.SemaphoreType.DMA((3,)),
        ],
        compiler_params=pltpu.CompilerParams(vmem_limit_bytes=48 * 1024 * 1024),
        name="lattice",
    )(parity, bias_out, own, b, a, target, *mats)


def gather_sum(x, axes):
    peers = lax.axis_size(axes)
    copies = jnp.broadcast_to(x[None], (peers,) + x.shape)
    return jnp.sum(lax.all_to_all(copies, axes, 0, 0, tiled=True), axis=0)


def body(populations, target_density, weight_in, bias_in, weight_out, bias_out):
    gx, gy = ("zh", "zl", "x", "yh"), ("yl", "c")
    nx, ny = lax.axis_size(gx), lax.axis_size(gy)
    mats = prep(weight_in, bias_in, weight_out)
    last = populations[:, :, 14:16, :].reshape(Q, 4, NZ)
    first = populations[:, :, 0:2, :].reshape(Q, 4, NZ)
    before = lax.ppermute(last, gy, [(j, (j + 1) % ny) for j in range(ny)])
    after = lax.ppermute(first, gy, [((j + 1) % ny, j) for j in range(ny)])
    own = jnp.concatenate(
        [
            before[:, 0:2],
            populations[:, 0],
            after[:, 0:2],
            before[:, 2:4],
            populations[:, 1],
            after[:, 2:4],
        ],
        axis=1,
    )
    pair = [(i, i ^ 1) for i in range(nx)]
    cross = [(i, (i + 1) % nx if i % 2 else (i - 1) % nx) for i in range(nx)]
    a = lax.ppermute(own, gx, pair)
    b = lax.ppermute(own, gx, cross)
    parity = (lax.axis_index("yh") % 2).astype(jnp.int32).reshape(1)
    moments, grads = main(parity, bias_out, own, a, b, target_density, mats)
    grads = gather_sum(grads, ("yh", "yl", "c"))
    grads = gather_sum(grads, ("zl", "x"))
    grads = lax.psum(grads, "zh")
    return (moments, *unpack(grads))


def solution(mesh):
    fine = Mesh(mesh.devices.reshape(4, 4, 4, 2, 2, 2), ("zh", "zl", "x", "yh", "yl", "c"))
    gx, gy = ("zh", "zl", "x", "yh"), ("yl", "c")
    placed = (P(None, gx, gy, None), P(gx, gy, None), P(), P(), P(), P())
    return jax.shard_map(
        body,
        mesh=fine,
        in_specs=placed,
        out_specs=(P(None, gx, gy, None), P(), P(), P(), P()),
        check_vma=False,
    )
```

```python
import math

import jax
import jax.numpy as jnp
from jax import lax
from jax.experimental import pallas as pl
from jax.experimental.pallas import tpu as pltpu
from jax.sharding import Mesh, PartitionSpec as P

velocity_table = (
    (0, 0, 0),
    (1, 0, 0),
    (-1, 0, 0),
    (0, 1, 0),
    (0, -1, 0),
    (0, 0, 1),
    (0, 0, -1),
    (1, 1, 0),
    (-1, -1, 0),
    (1, -1, 0),
    (-1, 1, 0),
    (1, 0, 1),
    (-1, 0, -1),
    (1, 0, -1),
    (-1, 0, 1),
    (0, 1, 1),
    (0, -1, -1),
    (0, 1, -1),
    (0, -1, 1),
)
lattice_weights = (1.0 / 3.0,) + (1.0 / 18.0,) * 6 + (1.0 / 36.0,) * 12
input_scale = 8.0
output_scale = 0.05
relax_time = 0.8

Q = 19
H = 32
NZ = 256
W1 = 20
W2 = 18
G1 = 2 * W1 // 8
G2 = 4 * W2 // 8
PG = (2, 7)
MARGIN = 8
SP = 8
QS = 20 * SP
HS = H * SP
MSG = 344
F32 = jnp.float32
BF16 = jnp.bfloat16
MIB = 1024 * 1024

to_right = [(q, -1) for q in range(19) if velocity_table[q][0] >= 0]
to_right += [(q, 0) for q in range(19) if velocity_table[q][0] == 1]
to_left = [(q, 2) for q in range(19) if velocity_table[q][0] <= 0]
to_left += [(q, 1) for q in range(19) if velocity_table[q][0] == -1]


def split(x):
    hi = x.astype(BF16)
    lo = (x - hi.astype(F32)).astype(BF16)
    return hi, lo


def mm(a, b):
    return lax.dot_general(a, b, (((1,), (0,)), ((), ())), preferred_element_type=F32)


def mm_nt(a, b):
    return lax.dot_general(a, b, (((1,), (1,)), ((), ())), preferred_element_type=F32)


def prep_kernel(win_ref, bin_ref, wout_ref, lin_ref, lint_ref, lout_ref, loutt_ref):
    hp = lax.Precision.HIGHEST
    nt = (((1,), (1,)), ((), ()))
    eq = (
        lax.broadcasted_iota(jnp.int32, (QS, Q), 0) // SP
        == lax.broadcasted_iota(jnp.int32, (QS, Q), 1)
    ).astype(F32)
    eh = (
        lax.broadcasted_iota(jnp.int32, (HS, H), 0) // SP
        == lax.broadcasted_iota(jnp.int32, (HS, H), 1)
    ).astype(F32)
    rq = lax.broadcasted_iota(jnp.int32, (QS, HS), 0)
    rh = lax.broadcasted_iota(jnp.int32, (QS, HS), 1)
    mask_qh = (rq % SP) == (rh % SP)
    ch = lax.broadcasted_iota(jnp.int32, (HS, QS), 0)
    cq = lax.broadcasted_iota(jnp.int32, (HS, QS), 1)
    mask_hq = (ch % SP) == (cq % SP)

    t_in = lax.dot_general(eq, win_ref[...] * input_scale, (((1,), (0,)), ((), ())), precision=hp, preferred_element_type=F32)
    t_out = lax.dot_general(eq, wout_ref[...] * output_scale, nt, precision=hp, preferred_element_type=F32)
    is_bias = lax.broadcasted_iota(jnp.int32, (QS, H), 0) >= Q * SP
    t_inb = jnp.where(is_bias, jnp.broadcast_to(bin_ref[...], (QS, H)), t_in)

    def put(ref, a, b, mask):
        full = lax.dot_general(a, b, nt, precision=hp, preferred_element_type=F32)
        hi, lo = split(jnp.where(mask, full, 0.0))
        n = full.shape[1]
        ref[:, 0:n] = hi
        ref[:, n : 2 * n] = hi
        ref[:, 2 * n : 3 * n] = lo

    put(lin_ref, eh, t_inb, mask_hq)
    put(lint_ref, t_in, eh, mask_qh)
    put(lout_ref, t_out, eh, mask_qh)
    put(loutt_ref, eh, t_out, mask_hq)


def equilibrium_parts(f):
    density = f[0]
    for q in range(1, Q):
        density = density + f[q]
    momentum = []
    for a in range(3):
        plus = None
        minus = None
        for q in range(Q):
            c = velocity_table[q][a]
            if c == 1:
                plus = f[q] if plus is None else plus + f[q]
            elif c == -1:
                minus = f[q] if minus is None else minus + f[q]
        momentum.append(plus - minus)
    return density, momentum


def project(q, m):
    out = None
    for a in range(3):
        c = velocity_table[q][a]
        if c == 0:
            continue
        if out is None:
            out = m[a] if c == 1 else -m[a]
        else:
            out = out + m[a] if c == 1 else out - m[a]
    return out


def excess_of(f):
    density, m = equilibrium_parts(f)
    base = density - 1.5 * (m[0] * m[0] + m[1] * m[1] + m[2] * m[2])
    excess = [f[0] - lattice_weights[0] * base]
    for q in range(1, Q, 2):
        w = lattice_weights[q]
        cm = project(q, m)
        even = w * (base + 4.5 * (cm * cm))
        odd = (3.0 * w) * cm
        excess.append(f[q] - (even + odd))
        excess.append(f[q + 1] - (even - odd))
    return excess, m


def rows8(x, q):
    return x[q * SP : (q + 1) * SP, :]


def collide(f, lin_ref, lout_ref, bout_ref, save_x, save_h):
    excess, m = excess_of(f)
    x = jnp.concatenate(excess + [jnp.ones((SP, NZ), F32)], axis=0)
    xhi, xlo = split(x)
    save_x(xhi, xlo)
    pre = mm(lin_ref[...], jnp.concatenate([xhi, xlo, xhi], axis=0))
    hid = jnp.tanh(pre)
    hhi, hlo = split(hid)
    save_h(hhi, hlo)
    corr = mm(lout_ref[...], jnp.concatenate([hhi, hlo, hhi], axis=0))
    out = []
    for q in range(Q):
        out.append(f[q] - excess[q] * (1.0 / relax_time) + (rows8(corr, q) + output_scale * bout_ref[q]))
    return out, m


def zroll(x, step):
    if step == 0:
        return x
    return pltpu.roll(x, step % NZ, 1)


def first_kernel(
    parity_ref,
    bout_ref,
    pop_ref,
    before_ref,
    after_ref,
    lin_ref,
    lout_ref,
    msg_a_ref,
    msg_b_ref,
    c1_ref,
    x1_ref,
    h1_ref,
    fs,
):
    for x in range(2):
        fs[:, W1 * x : W1 * x + 2, :] = before_ref[:, 2 * x : 2 * x + 2, :]
        fs[:, W1 * x + 2 : W1 * x + 18, :] = pop_ref[:, x]
        fs[:, W1 * x + 18 : W1 * x + 20, :] = after_ref[:, 2 * x : 2 * x + 2, :]
    for g in range(G1):
        f = [fs[q, 8 * g : 8 * g + 8, :] for q in range(Q)]

        def save_x(hi, lo):
            x1_ref[g, 0:QS, :] = hi
            x1_ref[g, QS : 2 * QS, :] = lo

        def save_h(hi, lo):
            h1_ref[g, 0:HS, :] = hi
            h1_ref[g, HS : 2 * HS, :] = lo

        out, _m = collide(f, lin_ref, lout_ref, bout_ref, save_x, save_h)
        for q in range(Q):
            c1_ref[q, 8 * g : 8 * g + 8, :] = zroll(out[q], velocity_table[q][2])
    odd = parity_ref[0] == 1

    def piece(q, plane):
        start = W1 * (plane - velocity_table[q][0]) + 1 - velocity_table[q][1]
        return c1_ref[q, start : start + W2, :]

    for k in range(Q):
        q, plane = to_right[k]
        right = piece(q, plane + 2)
        q, plane = to_left[k]
        left = piece(q, plane - 2)
        msg_a_ref[W2 * k : W2 * k + W2, :] = jnp.where(odd, left, right)
        msg_b_ref[W2 * k : W2 * k + W2, :] = jnp.where(odd, right, left)
    msg_a_ref[W2 * Q :, :] = jnp.zeros((MSG - W2 * Q, NZ), F32)
    msg_b_ref[W2 * Q :, :] = jnp.zeros((MSG - W2 * Q, NZ), F32)


def second_kernel(
    parity_ref,
    bout_ref,
    c1_ref,
    msg_a_ref,
    msg_b_ref,
    target_ref,
    lin_ref,
    lout_ref,
    moments_ref,
    r_ref,
    x2_ref,
    h2_ref,
    m2_ref,
    a1,
    c2,
):
    odd = parity_ref[0] == 1
    for k in range(Q):
        rows = slice(W2 * k, W2 * k + W2)
        msg_a = msg_a_ref[rows, :]
        msg_b = msg_b_ref[rows, :]
        q, plane = to_right[k]
        a1[q, W2 * (plane + 1) : W2 * (plane + 2), :] = jnp.where(odd, msg_a, msg_b)
        q, plane = to_left[k]
        a1[q, W2 * (plane + 1) : W2 * (plane + 2), :] = jnp.where(odd, msg_b, msg_a)
    for q in range(Q):
        for plane in range(-1, 3):
            source = plane - velocity_table[q][0]
            if source in (0, 1):
                start = W1 * source + 1 - velocity_table[q][1]
                a1[q, W2 * (plane + 1) : W2 * (plane + 2), :] = c1_ref[q, start : start + W2, :]
    for g in range(G2):
        f = [a1[q, 8 * g : 8 * g + 8, :] for q in range(Q)]

        def save_x(hi, lo):
            if PG[0] <= g < PG[1]:
                x2_ref[g - PG[0], 0:QS, :] = hi
                x2_ref[g - PG[0], QS : 2 * QS, :] = lo

        def save_h(hi, lo):
            h2_ref[g, 0:HS, :] = hi
            h2_ref[g, HS : 2 * HS, :] = lo

        out, m = collide(f, lin_ref, lout_ref, bout_ref, save_x, save_h)
        for a in range(3):
            m2_ref[g, a] = m[a]
        for q in range(Q):
            c2[q, 8 * g : 8 * g + 8, :] = zroll(out[q], velocity_table[q][2])
    residual_scale = 1.0 / math.sqrt(256 * 64 * 256)
    for x in range(2):
        for half in range(2):
            first = W2 * (x + 1) + 1 + 8 * half
            f = []
            for q in range(Q):
                start = first - W2 * velocity_table[q][0] - velocity_table[q][1]
                f.append(c2[q, start : start + 8, :])
            density, m = equilibrium_parts(f)
            moments_ref[0, x, 8 * half : 8 * half + 8, :] = density
            for a in range(3):
                moments_ref[a + 1, x, 8 * half : 8 * half + 8, :] = m[a]
            r = (density - target_ref[x, 8 * half : 8 * half + 8, :]) * residual_scale
            r_ref[16 * x + 8 * half : 16 * x + 8 * half + 8, :] = r


def third_kernel(
    parity_ref,
    r_ref,
    r_b_ref,
    r_a_ref,
    x1_ref,
    h1_ref,
    x2_ref,
    h2_ref,
    m2_ref,
    lint_ref,
    loutt_ref,
    grads_ref,
    rs,
    g1s,
    acc_in,
    acc_out,
    acc_b,
):
    odd = parity_ref[0] == 1
    rs[...] = jnp.zeros_like(rs)
    g1s[...] = jnp.zeros_like(g1s)
    acc_in[...] = jnp.zeros_like(acc_in)
    acc_out[...] = jnp.zeros_like(acc_out)
    acc_b[...] = jnp.zeros_like(acc_b)
    r_a, r_b = r_a_ref[...], r_b_ref[...]
    parts = (jnp.where(odd, r_a, r_b), r_ref[...], jnp.where(odd, r_b, r_a))
    for i in range(6):
        first = MARGIN + W2 * i + 1
        for half in range(2):
            at = 16 * (i % 2) + 8 * half
            r = parts[i // 2][at : at + 8, :]
            rows = slice(first + 8 * half, first + 8 * half + 8)
            rs[0, rows, :] = r
            rs[1, rows, :] = zroll(r, -1)
            rs[2, rows, :] = zroll(r, 1)

    def hidden_pull(gq, hhi, hlo):
        gs = jnp.concatenate(gq + [jnp.zeros((SP, NZ), F32)], axis=0)
        ghi, glo = split(gs)
        dh = mm(loutt_ref[...], jnp.concatenate([ghi, glo, ghi], axis=0))
        hid = hhi.astype(F32) + hlo.astype(F32)
        return gs, dh * (1.0 - hid * hid)

    def add_params(gs, dpre, xhi, xlo, hhi, hlo):
        ghi, glo = split(gs)
        dhi, dlo = split(dpre)
        acc_in[...] += mm_nt(
            jnp.concatenate([xhi, xlo, xhi], axis=1), jnp.concatenate([dhi, dhi, dlo], axis=1)
        )
        acc_out[...] += mm_nt(
            jnp.concatenate([ghi, glo, ghi], axis=1), jnp.concatenate([hhi, hhi, hlo], axis=1)
        )
        acc_b[...] += gs

    def keep(x, lo, hi):
        if lo == 0 and hi == SP:
            return x
        row = lax.broadcasted_iota(jnp.int32, x.shape, 0) % SP
        return jnp.where((row >= lo) & (row < hi), x, 0.0)

    for g in range(G2):
        gq = []
        for q in range(Q):
            cx, cy, cz = velocity_table[q]
            start = MARGIN + W2 + 8 * g + W2 * cx + cy
            gq.append(rs[{0: 0, 1: 1, -1: 2}[cz], start : start + 8, :])
        hhi = h2_ref[g, 0:HS, :]
        hlo = h2_ref[g, HS : 2 * HS, :]
        gs, dpre = hidden_pull(gq, hhi, hlo)
        if PG[0] <= g < PG[1]:
            lo = max(W2 - 8 * g, 0)
            hi = min(3 * W2 - 8 * g, SP)
            add_params(
                keep(gs, lo, hi),
                keep(dpre, lo, hi),
                x2_ref[g - PG[0], 0:QS, :],
                x2_ref[g - PG[0], QS : 2 * QS, :],
                hhi,
                hlo,
            )
        dhi, dlo = split(dpre)
        back = mm(lint_ref[...], jnp.concatenate([dhi, dlo, dhi], axis=0))
        m = [m2_ref[g, a] for a in range(3)]
        de = [rows8(back, q) - gq[q] * (1.0 / relax_time) for q in range(Q)]
        t = [lattice_weights[q] * de[q] for q in range(Q)]
        drho = t[0]
        for q in range(1, Q):
            drho = drho + t[q]
        u = [None] * Q
        for q in range(1, Q, 2):
            cm = 9.0 * project(q, m)
            u[q] = t[q] * (3.0 + cm)
            u[q + 1] = t[q + 1] * (3.0 - cm)
        dm = []
        for a in range(3):
            plus = None
            minus = None
            for q in range(Q):
                c = velocity_table[q][a]
                if c == 1:
                    plus = u[q] if plus is None else plus + u[q]
                elif c == -1:
                    minus = u[q] if minus is None else minus + u[q]
            dm.append(plus - minus - 3.0 * m[a] * drho)
        for q in range(Q):
            df = gq[q] + de[q] - drho
            if q:
                df = df - project(q, dm)
            df = zroll(df, -velocity_table[q][2])
            for plane in range(4):
                lo = max(W2 * plane, 8 * g)
                hi = min(W2 * plane + W2, 8 * g + 8)
                if lo < hi:
                    at = MARGIN + 1 + 2 * plane
                    g1s[q, at + lo : at + hi, :] = df[lo - 8 * g : hi - 8 * g, :]

    for g in range(G1):
        gq = []
        for q in range(Q):
            cx, cy, _cz = velocity_table[q]
            start = MARGIN + W1 + 8 * g + W1 * cx + cy
            gq.append(g1s[q, start : start + 8, :])
        hhi = h1_ref[g, 0:HS, :]
        hlo = h1_ref[g, HS : 2 * HS, :]
        gs, dpre = hidden_pull(gq, hhi, hlo)
        add_params(gs, dpre, x1_ref[g, 0:QS, :], x1_ref[g, QS : 2 * QS, :], hhi, hlo)

    hp = lax.Precision.HIGHEST
    rq = lax.broadcasted_iota(jnp.int32, (QS, HS), 0)
    rh = lax.broadcasted_iota(jnp.int32, (QS, HS), 1)
    mask = (rq % SP) == (rh % SP)
    fold = (
        lax.broadcasted_iota(jnp.int32, (HS, H), 0) // SP
        == lax.broadcasted_iota(jnp.int32, (HS, H), 1)
    ).astype(F32)

    def trace(acc):
        kept = jnp.where(mask, acc[...], 0.0).reshape(20, SP, HS).sum(axis=1)
        return lax.dot_general(
            kept, fold, (((1,), (0,)), ((), ())), precision=hp, preferred_element_type=F32
        )

    q_index = lax.broadcasted_iota(jnp.int32, (20, H), 0)
    d_in = trace(acc_in) * jnp.where(q_index < Q, input_scale, 1.0)
    d_out = trace(acc_out) * output_scale
    d_b = acc_b[...].reshape(20, SP, NZ).sum(axis=1).sum(axis=1, keepdims=True) * output_scale
    grads_ref[...] = jnp.zeros_like(grads_ref)
    grads_ref[0:10, 0:H] = d_in[0:10]
    grads_ref[0:10, H : 2 * H] = d_in[10:20]
    grads_ref[0:10, 2 * H : 3 * H] = d_out[0:10]
    grads_ref[0:10, 3 * H : 4 * H] = d_out[10:20]
    for i in range(4):
        grads_ref[10:15, i : i + 1] = d_b[5 * i : 5 * i + 5]


def unpack(grads):
    d_in = jnp.concatenate([grads[0:10, 0:H], grads[0:10, H : 2 * H]], axis=0)
    d_out = jnp.concatenate([grads[0:10, 2 * H : 3 * H], grads[0:10, 3 * H :]], axis=0)
    d_b = grads[10:15, 0:4].T.reshape(20)
    return d_in[0:Q], d_in[Q], d_out[0:Q].T, d_b[0:Q]


def prep(weight_in, bias_in, weight_out):
    return pl.pallas_call(
        prep_kernel,
        out_shape=(
            jax.ShapeDtypeStruct((HS, 3 * QS), BF16),
            jax.ShapeDtypeStruct((QS, 3 * HS), BF16),
            jax.ShapeDtypeStruct((QS, 3 * HS), BF16),
            jax.ShapeDtypeStruct((HS, 3 * QS), BF16),
        ),
        compiler_params=pltpu.CompilerParams(vmem_limit_bytes=24 * 1024 * 1024),
        name="prep",
    )(weight_in, bias_in.reshape(1, H), weight_out)


VMEM = pl.BlockSpec(memory_space=pltpu.VMEM)
SMEM = pl.BlockSpec(memory_space=pltpu.SMEM)


def shape(*dims, kind=F32):
    return jax.ShapeDtypeStruct(dims, kind)


def first(parity, bias_out, populations, before, after, lin, lout):
    return pl.pallas_call(
        first_kernel,
        out_shape=(
            shape(MSG, NZ),
            shape(MSG, NZ),
            shape(Q, 2 * W1, NZ),
            shape(G1, 2 * QS, NZ, kind=BF16),
            shape(G1, 2 * HS, NZ, kind=BF16),
        ),
        in_specs=[SMEM, SMEM] + [VMEM] * 5,
        out_specs=(VMEM,) * 5,
        scratch_shapes=[pltpu.VMEM((Q, 2 * W1, NZ), F32)],
        compiler_params=pltpu.CompilerParams(vmem_limit_bytes=24 * MIB),
        name="first",
    )(parity, bias_out, populations, before, after, lin, lout)


def second(parity, bias_out, c1, msg_a, msg_b, target, lin, lout):
    return pl.pallas_call(
        second_kernel,
        out_shape=(
            shape(4, 2, 16, NZ),
            shape(32, NZ),
            shape(PG[1] - PG[0], 2 * QS, NZ, kind=BF16),
            shape(G2, 2 * HS, NZ, kind=BF16),
            shape(G2, 3, SP, NZ),
        ),
        in_specs=[SMEM, SMEM] + [VMEM] * 6,
        out_specs=(VMEM,) * 5,
        scratch_shapes=[pltpu.VMEM((Q, 4 * W2, NZ), F32)] * 2,
        compiler_params=pltpu.CompilerParams(vmem_limit_bytes=24 * MIB),
        name="second",
    )(parity, bias_out, c1, msg_a, msg_b, target, lin, lout)


def third(parity, r, r_b, r_a, x1, h1, x2, h2, m2, lint, loutt):
    return pl.pallas_call(
        third_kernel,
        out_shape=shape(16, 128),
        in_specs=[SMEM] + [VMEM] * 10,
        out_specs=VMEM,
        scratch_shapes=[
            pltpu.VMEM((3, 2 * MARGIN + 6 * W2 + 4, NZ), F32),
            pltpu.VMEM((Q, 2 * MARGIN + 4 * W1, NZ), F32),
            pltpu.VMEM((QS, HS), F32),
            pltpu.VMEM((QS, HS), F32),
            pltpu.VMEM((QS, NZ), F32),
        ],
        compiler_params=pltpu.CompilerParams(vmem_limit_bytes=24 * MIB),
        name="third",
    )(parity, r, r_b, r_a, x1, h1, x2, h2, m2, lint, loutt)


def gather_sum(x, axes):
    peers = lax.axis_size(axes)
    copies = jnp.broadcast_to(x[None], (peers,) + x.shape)
    return jnp.sum(lax.all_to_all(copies, axes, 0, 0, tiled=True), axis=0)


def body(populations, target_density, weight_in, bias_in, weight_out, bias_out):
    gx, gy = ("zh", "zl", "x", "yh"), ("yl", "c")
    nx, ny = lax.axis_size(gx), lax.axis_size(gy)
    lin, lint, lout, loutt = prep(weight_in, bias_in, weight_out)
    last = populations[:, :, 14:16, :].reshape(Q, 4, NZ)
    start = populations[:, :, 0:2, :].reshape(Q, 4, NZ)
    before = lax.ppermute(last, gy, [(j, (j + 1) % ny) for j in range(ny)])
    after = lax.ppermute(start, gy, [((j + 1) % ny, j) for j in range(ny)])
    pair = [(i, i ^ 1) for i in range(nx)]
    cross = [(i, (i + 1) % nx if i % 2 else (i - 1) % nx) for i in range(nx)]
    parity = (lax.axis_index("yh") % 2).astype(jnp.int32).reshape(1)
    msg_a, msg_b, c1, x1, h1 = first(parity, bias_out, populations, before, after, lin, lout)
    got_a = lax.ppermute(msg_a, gx, pair)
    got_b = lax.ppermute(msg_b, gx, cross)
    moments, r, x2, h2, m2 = second(
        parity, bias_out, c1, got_a, got_b, target_density, lin, lout
    )
    r_a = lax.ppermute(r, gx, pair)
    r_b = lax.ppermute(r, gx, cross)
    grads = third(parity, r, r_b, r_a, x1, h1, x2, h2, m2, lint, loutt)
    grads = gather_sum(grads, ("yh", "yl", "c"))
    grads = gather_sum(grads, ("zl", "x"))
    grads = lax.psum(grads, "zh")
    return (moments, *unpack(grads))


def solution(mesh):
    fine = Mesh(mesh.devices.reshape(4, 4, 4, 2, 2, 2), ("zh", "zl", "x", "yh", "yl", "c"))
    gx, gy = ("zh", "zl", "x", "yh"), ("yl", "c")
    placed = (P(None, gx, gy, None), P(gx, gy, None), P(), P(), P(), P())
    return jax.shard_map(
        body,
        mesh=fine,
        in_specs=placed,
        out_specs=(P(None, gx, gy, None), P(), P(), P(), P()),
        check_vma=False,
    )
```

```python
import math

import jax
import jax.numpy as jnp
from jax import lax
from jax.experimental import pallas as pl
from jax.experimental.pallas import tpu as pltpu
from jax.sharding import Mesh, PartitionSpec as P

velocity_table = (
    (0, 0, 0),
    (1, 0, 0),
    (-1, 0, 0),
    (0, 1, 0),
    (0, -1, 0),
    (0, 0, 1),
    (0, 0, -1),
    (1, 1, 0),
    (-1, -1, 0),
    (1, -1, 0),
    (-1, 1, 0),
    (1, 0, 1),
    (-1, 0, -1),
    (1, 0, -1),
    (-1, 0, 1),
    (0, 1, 1),
    (0, -1, -1),
    (0, 1, -1),
    (0, -1, 1),
)
lattice_weights = (1.0 / 3.0,) + (1.0 / 18.0,) * 6 + (1.0 / 36.0,) * 12
input_scale = 8.0
output_scale = 0.05
relax_time = 0.8

Q = 19
H = 32
NZ = 256
W1 = 20
W2 = 18
G1 = 2 * W1 // 8
G2 = 4 * W2 // 8
PG = (2, 7)
MARGIN = 8
SP = 8
QS = 20 * SP
HS = H * SP
MSG = 344
F32 = jnp.float32
BF16 = jnp.bfloat16
MIB = 1024 * 1024
B1, B2, B4, B5 = 5, 9, 3, 3

to_right = [(q, -1) for q in range(19) if velocity_table[q][0] >= 0]
to_right += [(q, 0) for q in range(19) if velocity_table[q][0] == 1]
to_left = [(q, 2) for q in range(19) if velocity_table[q][0] <= 0]
to_left += [(q, 1) for q in range(19) if velocity_table[q][0] == -1]


def split(x):
    hi = x.astype(BF16)
    lo = (x - hi.astype(F32)).astype(BF16)
    return hi, lo


def mm(a, b):
    return lax.dot_general(a, b, (((1,), (0,)), ((), ())), preferred_element_type=F32)


def mm_nt(a, b):
    return lax.dot_general(a, b, (((1,), (1,)), ((), ())), preferred_element_type=F32)


def expanded(packed_ref):
    hp = lax.Precision.HIGHEST
    nn = (((1,), (0,)), ((), ()))
    eq = (
        lax.broadcasted_iota(jnp.int32, (QS, 20), 0) // SP
        == lax.broadcasted_iota(jnp.int32, (QS, 20), 1)
    ).astype(F32)
    eh = (
        lax.broadcasted_iota(jnp.int32, (HS, H), 0) // SP
        == lax.broadcasted_iota(jnp.int32, (HS, H), 1)
    ).astype(F32)
    row = lax.broadcasted_iota(jnp.int32, (20, H), 0)
    w_in = packed_ref[0:20, :] * jnp.where(row < Q, input_scale, 1.0)
    w_out = jnp.where(row < Q, packed_ref[20:40, :] * output_scale, 0.0)
    t_in = lax.dot_general(eq, w_in, nn, precision=hp, preferred_element_type=F32)
    t_out = lax.dot_general(eq, w_out, nn, precision=hp, preferred_element_type=F32)
    return eh, t_in, t_out


def put(ref, a, b):
    hp = lax.Precision.HIGHEST
    nt = (((1,), (1,)), ((), ()))
    full = lax.dot_general(a, b, nt, precision=hp, preferred_element_type=F32)
    m, n = full.shape
    row = lax.broadcasted_iota(jnp.int32, (m, n), 0)
    column = lax.broadcasted_iota(jnp.int32, (m, n), 1)
    hi, lo = split(jnp.where((row % SP) == (column % SP), full, 0.0))
    ref[:, 0:n] = hi
    ref[:, n : 2 * n] = hi
    ref[:, 2 * n : 3 * n] = lo


def prep_kernel(packed_ref, lin_ref, lout_ref, bout_ref):
    eh, t_in, t_out = expanded(packed_ref)
    put(lin_ref, eh, t_in)
    put(lout_ref, t_out, eh)
    pick = (
        lax.broadcasted_iota(jnp.int32, (QS, H), 0) // SP
        == lax.broadcasted_iota(jnp.int32, (QS, H), 1)
    ).astype(F32)
    bias = jnp.sum(pick * (packed_ref[39:40, :] * output_scale), axis=1, keepdims=True)
    bout_ref[...] = jnp.broadcast_to(bias, (QS, NZ))


def middle_kernel(after_first, packed_ref, target_in, lint_ref, loutt_ref, target_ref):
    target_ref[...] = target_in[...]
    eh, t_in, t_out = expanded(packed_ref)
    is_bias = lax.broadcasted_iota(jnp.int32, (QS, H), 0) >= Q * SP
    put(lint_ref, jnp.where(is_bias, 0.0, t_in), eh)
    put(loutt_ref, eh, t_out)


def equilibrium_parts(f):
    density = f[0]
    for q in range(1, Q):
        density = density + f[q]
    momentum = []
    for a in range(3):
        plus = None
        minus = None
        for q in range(Q):
            c = velocity_table[q][a]
            if c == 1:
                plus = f[q] if plus is None else plus + f[q]
            elif c == -1:
                minus = f[q] if minus is None else minus + f[q]
        momentum.append(plus - minus)
    return density, momentum


def project(q, m):
    out = None
    for a in range(3):
        c = velocity_table[q][a]
        if c == 0:
            continue
        if out is None:
            out = m[a] if c == 1 else -m[a]
        else:
            out = out + m[a] if c == 1 else out - m[a]
    return out


def excess_of(f):
    density, m = equilibrium_parts(f)
    base = density - 1.5 * (m[0] * m[0] + m[1] * m[1] + m[2] * m[2])
    excess = [f[0] - lattice_weights[0] * base]
    for q in range(1, Q, 2):
        w = lattice_weights[q]
        cm = project(q, m)
        even = w * (base + 4.5 * (cm * cm))
        odd = (3.0 * w) * cm
        excess.append(f[q] - (even + odd))
        excess.append(f[q + 1] - (even - odd))
    return excess, m


def rows8(x, q):
    return x[q * SP : (q + 1) * SP, :]


def batches(groups, size):
    return [range(g, min(g + size, groups)) for g in range(0, groups, size)]


def lanes(parts):
    return parts[0] if len(parts) == 1 else jnp.concatenate(parts, axis=1)


def block(x, i):
    return x[:, i * NZ : (i + 1) * NZ]


def stack3(hi, lo):
    return jnp.concatenate([hi, lo, hi], axis=0)


def collide(fs, lin_ref, lout_ref, bout_ref, save_x, save_h):
    excesses, ms, his, los = [], [], [], []
    for i, f in enumerate(fs):
        excess, m = excess_of(f)
        x = jnp.concatenate(excess + [jnp.ones((SP, NZ), F32)], axis=0)
        xhi, xlo = split(x)
        save_x(i, xhi, xlo)
        excesses.append(excess)
        ms.append(m)
        his.append(xhi)
        los.append(xlo)
    pre = mm(lin_ref[...], stack3(lanes(his), lanes(los)))
    hhi, hlo = split(jnp.tanh(pre))
    for i in range(len(fs)):
        save_h(i, block(hhi, i), block(hlo, i))
    corr = mm(lout_ref[...], stack3(hhi, hlo))
    outs = []
    for i, f in enumerate(fs):
        out = []
        for q in range(Q):
            bias = bout_ref[q * SP : (q + 1) * SP, :]
            add = block(rows8(corr, q), i) + bias
            out.append(f[q] - excesses[i][q] * (1.0 / relax_time) + add)
        outs.append(out)
    return outs, ms


def zroll(x, step):
    if step == 0:
        return x
    return pltpu.roll(x, step % NZ, 1)


def edges_kernel(pop_hbm, last_ref, start_ref, pop_ref, sem):
    copy = pltpu.make_async_copy(pop_hbm, pop_ref, sem)
    copy.start()
    copy.wait()
    for x in range(2):
        last_ref[:, 2 * x : 2 * x + 2, :] = pop_ref[:, x, 14:16, :]
        start_ref[:, 2 * x : 2 * x + 2, :] = pop_ref[:, x, 0:2, :]


def first_kernel(
    parity_ref,
    bout_ref,
    pop_ref,
    before_ref,
    after_ref,
    lin_ref,
    lout_ref,
    msg_a_ref,
    msg_b_ref,
    c1_ref,
    x1_ref,
    h1_ref,
    fs,
):
    for x in range(2):
        fs[:, W1 * x : W1 * x + 2, :] = before_ref[:, 2 * x : 2 * x + 2, :]
        fs[:, W1 * x + 2 : W1 * x + 18, :] = pop_ref[:, x]
        fs[:, W1 * x + 18 : W1 * x + 20, :] = after_ref[:, 2 * x : 2 * x + 2, :]
    for batch in batches(G1, B1):
        f = [[fs[q, 8 * g : 8 * g + 8, :] for q in range(Q)] for g in batch]

        def save_x(i, hi, lo):
            x1_ref[batch[i], 0:QS, :] = hi
            x1_ref[batch[i], QS : 2 * QS, :] = lo

        def save_h(i, hi, lo):
            h1_ref[batch[i], 0:HS, :] = hi
            h1_ref[batch[i], HS : 2 * HS, :] = lo

        outs, _m = collide(f, lin_ref, lout_ref, bout_ref, save_x, save_h)
        for g, out in zip(batch, outs):
            for q in range(Q):
                c1_ref[q, 8 * g : 8 * g + 8, :] = zroll(out[q], velocity_table[q][2])
    odd = parity_ref[0] == 1

    def piece(q, plane):
        start = W1 * (plane - velocity_table[q][0]) + 1 - velocity_table[q][1]
        return c1_ref[q, start : start + W2, :]

    for k in range(Q):
        q, plane = to_right[k]
        right = piece(q, plane + 2)
        q, plane = to_left[k]
        left = piece(q, plane - 2)
        msg_a_ref[W2 * k : W2 * k + W2, :] = jnp.where(odd, left, right)
        msg_b_ref[W2 * k : W2 * k + W2, :] = jnp.where(odd, right, left)
    msg_a_ref[W2 * Q :, :] = jnp.zeros((MSG - W2 * Q, NZ), F32)
    msg_b_ref[W2 * Q :, :] = jnp.zeros((MSG - W2 * Q, NZ), F32)


def second_kernel(
    parity_ref,
    bout_ref,
    c1_ref,
    msg_a_ref,
    msg_b_ref,
    target_ref,
    lin_ref,
    lout_ref,
    moments_ref,
    r_ref,
    x2_ref,
    h2_ref,
    m2_ref,
    a1,
    c2,
):
    odd = parity_ref[0] == 1
    for k in range(Q):
        rows = slice(W2 * k, W2 * k + W2)
        msg_a = msg_a_ref[rows, :]
        msg_b = msg_b_ref[rows, :]
        q, plane = to_right[k]
        a1[q, W2 * (plane + 1) : W2 * (plane + 2), :] = jnp.where(odd, msg_a, msg_b)
        q, plane = to_left[k]
        a1[q, W2 * (plane + 1) : W2 * (plane + 2), :] = jnp.where(odd, msg_b, msg_a)
    for q in range(Q):
        for plane in range(-1, 3):
            source = plane - velocity_table[q][0]
            if source in (0, 1):
                start = W1 * source + 1 - velocity_table[q][1]
                a1[q, W2 * (plane + 1) : W2 * (plane + 2), :] = c1_ref[q, start : start + W2, :]
    for batch in batches(G2, B2):
        f = [[a1[q, 8 * g : 8 * g + 8, :] for q in range(Q)] for g in batch]

        def save_x(i, hi, lo):
            if PG[0] <= batch[i] < PG[1]:
                x2_ref[batch[i] - PG[0], 0:QS, :] = hi
                x2_ref[batch[i] - PG[0], QS : 2 * QS, :] = lo

        def save_h(i, hi, lo):
            h2_ref[batch[i], 0:HS, :] = hi
            h2_ref[batch[i], HS : 2 * HS, :] = lo

        outs, ms = collide(f, lin_ref, lout_ref, bout_ref, save_x, save_h)
        for g, out, m in zip(batch, outs, ms):
            for a in range(3):
                m2_ref[g, a] = m[a]
            for q in range(Q):
                c2[q, 8 * g : 8 * g + 8, :] = zroll(out[q], velocity_table[q][2])
    residual_scale = 1.0 / math.sqrt(256 * 64 * 256)
    for x in range(2):
        for half in range(2):
            first = W2 * (x + 1) + 1 + 8 * half
            f = []
            for q in range(Q):
                start = first - W2 * velocity_table[q][0] - velocity_table[q][1]
                f.append(c2[q, start : start + 8, :])
            density, m = equilibrium_parts(f)
            moments_ref[0, x, 8 * half : 8 * half + 8, :] = density
            for a in range(3):
                moments_ref[a + 1, x, 8 * half : 8 * half + 8, :] = m[a]
            r = (density - target_ref[x, 8 * half : 8 * half + 8, :]) * residual_scale
            r_ref[16 * x + 8 * half : 16 * x + 8 * half + 8, :] = r


def third_kernel(
    parity_ref,
    r_ref,
    r_b_ref,
    r_a_ref,
    x1_ref,
    h1_ref,
    x2_ref,
    h2_ref,
    m2_ref,
    lint_ref,
    loutt_ref,
    grads_ref,
    rs,
    g1s,
    acc_in,
    acc_out,
    acc_b,
):
    odd = parity_ref[0] == 1
    rs[...] = jnp.zeros_like(rs)
    g1s[...] = jnp.zeros_like(g1s)
    acc_in[...] = jnp.zeros_like(acc_in)
    acc_out[...] = jnp.zeros_like(acc_out)
    acc_b[...] = jnp.zeros_like(acc_b)
    r_a, r_b = r_a_ref[...], r_b_ref[...]
    parts = (jnp.where(odd, r_a, r_b), r_ref[...], jnp.where(odd, r_b, r_a))
    for i in range(6):
        first = MARGIN + W2 * i + 1
        for half in range(2):
            at = 16 * (i % 2) + 8 * half
            r = parts[i // 2][at : at + 8, :]
            rows = slice(first + 8 * half, first + 8 * half + 8)
            rs[0, rows, :] = r
            rs[1, rows, :] = zroll(r, -1)
            rs[2, rows, :] = zroll(r, 1)

    def hidden_pull(gqs, h_ref, batch):
        gs, ghi, glo = [], [], []
        for gq in gqs:
            g = jnp.concatenate(gq + [jnp.zeros((SP, NZ), F32)], axis=0)
            hi, lo = split(g)
            gs.append(g)
            ghi.append(hi)
            glo.append(lo)
        dh = mm(loutt_ref[...], stack3(lanes(ghi), lanes(glo)))
        dpre = []
        for i, g in enumerate(batch):
            hid = h_ref[g, 0:HS, :].astype(F32) + h_ref[g, HS : 2 * HS, :].astype(F32)
            dpre.append(block(dh, i) * (1.0 - hid * hid))
        return gs, dpre

    def add_params(gs, dpre, x_ref, h_ref, x_at, h_at):
        ghi, glo = zip(*[split(g) for g in gs])
        dhi, dlo = zip(*[split(d) for d in dpre])
        xhi = [x_ref[g, 0:QS, :] for g in x_at]
        xlo = [x_ref[g, QS : 2 * QS, :] for g in x_at]
        hhi = [h_ref[g, 0:HS, :] for g in h_at]
        hlo = [h_ref[g, HS : 2 * HS, :] for g in h_at]
        xh, xl, dh, dl = lanes(xhi), lanes(xlo), lanes(dhi), lanes(dlo)
        both = mm_nt(jnp.concatenate([xh, xl], axis=0), dh)
        acc_in[...] += both[0:QS] + both[QS:] + mm_nt(xh, dl)
        gh, gl, hh, hl = lanes(ghi), lanes(glo), lanes(hhi), lanes(hlo)
        both = mm_nt(jnp.concatenate([gh, gl], axis=0), hh)
        acc_out[...] += both[0:QS] + both[QS:] + mm_nt(gh, hl)
        acc_b[...] += sum(gs[1:], gs[0])

    def keep(x, lo, hi):
        if lo == 0 and hi == SP:
            return x
        row = lax.broadcasted_iota(jnp.int32, x.shape, 0) % SP
        return jnp.where((row >= lo) & (row < hi), x, 0.0)

    for batch in batches(G2, B4):
        gqs = []
        for g in batch:
            gq = []
            for q in range(Q):
                cx, cy, cz = velocity_table[q]
                start = MARGIN + W2 + 8 * g + W2 * cx + cy
                gq.append(rs[{0: 0, 1: 1, -1: 2}[cz], start : start + 8, :])
            gqs.append(gq)
        gs, dpre = hidden_pull(gqs, h2_ref, batch)
        kept_g, kept_d, kept_at = [], [], []
        for i, g in enumerate(batch):
            if PG[0] <= g < PG[1]:
                lo = max(W2 - 8 * g, 0)
                hi = min(3 * W2 - 8 * g, SP)
                kept_g.append(keep(gs[i], lo, hi))
                kept_d.append(keep(dpre[i], lo, hi))
                kept_at.append(g)
        if kept_at:
            add_params(kept_g, kept_d, x2_ref, h2_ref, [g - PG[0] for g in kept_at], kept_at)
        dhi, dlo = split(lanes(dpre))
        back = mm(lint_ref[...], stack3(dhi, dlo))
        for i, g in enumerate(batch):
            m = [m2_ref[g, a] for a in range(3)]
            de = [block(rows8(back, q), i) - gqs[i][q] * (1.0 / relax_time) for q in range(Q)]
            t = [lattice_weights[q] * de[q] for q in range(Q)]
            drho = t[0]
            for q in range(1, Q):
                drho = drho + t[q]
            u = [None] * Q
            for q in range(1, Q, 2):
                cm = 9.0 * project(q, m)
                u[q] = t[q] * (3.0 + cm)
                u[q + 1] = t[q + 1] * (3.0 - cm)
            dm = []
            for a in range(3):
                plus = None
                minus = None
                for q in range(Q):
                    c = velocity_table[q][a]
                    if c == 1:
                        plus = u[q] if plus is None else plus + u[q]
                    elif c == -1:
                        minus = u[q] if minus is None else minus + u[q]
                dm.append(plus - minus - 3.0 * m[a] * drho)
            for q in range(Q):
                df = gqs[i][q] + de[q] - drho
                if q:
                    df = df - project(q, dm)
                df = zroll(df, -velocity_table[q][2])
                for plane in range(4):
                    lo = max(W2 * plane, 8 * g)
                    hi = min(W2 * plane + W2, 8 * g + 8)
                    if lo < hi:
                        at = MARGIN + 1 + 2 * plane
                        g1s[q, at + lo : at + hi, :] = df[lo - 8 * g : hi - 8 * g, :]

    for batch in batches(G1, B5):
        gqs = []
        for g in batch:
            gq = []
            for q in range(Q):
                cx, cy, _cz = velocity_table[q]
                start = MARGIN + W1 + 8 * g + W1 * cx + cy
                gq.append(g1s[q, start : start + 8, :])
            gqs.append(gq)
        gs, dpre = hidden_pull(gqs, h1_ref, batch)
        add_params(gs, dpre, x1_ref, h1_ref, batch, batch)

    hp = lax.Precision.HIGHEST
    rq = lax.broadcasted_iota(jnp.int32, (QS, HS), 0)
    rh = lax.broadcasted_iota(jnp.int32, (QS, HS), 1)
    mask = (rq % SP) == (rh % SP)
    fold = (
        lax.broadcasted_iota(jnp.int32, (HS, H), 0) // SP
        == lax.broadcasted_iota(jnp.int32, (HS, H), 1)
    ).astype(F32)

    def trace(acc):
        kept = jnp.where(mask, acc[...], 0.0).reshape(20, SP, HS).sum(axis=1)
        return lax.dot_general(
            kept, fold, (((1,), (0,)), ((), ())), precision=hp, preferred_element_type=F32
        )

    q_index = lax.broadcasted_iota(jnp.int32, (20, H), 0)
    d_in = trace(acc_in) * jnp.where(q_index < Q, input_scale, 1.0)
    d_out = trace(acc_out) * output_scale
    nt = (((1,), (1,)), ((), ()))
    b_row = lax.dot_general(
        jnp.full((1, NZ), output_scale, F32), acc_b[...], nt, precision=hp, preferred_element_type=F32
    )
    d_b = lax.dot_general(
        b_row,
        (
            lax.broadcasted_iota(jnp.int32, (QS, 20), 0) // SP
            == lax.broadcasted_iota(jnp.int32, (QS, 20), 1)
        ).astype(F32),
        (((1,), (0,)), ((), ())),
        precision=hp,
        preferred_element_type=F32,
    )
    grads_ref[...] = jnp.zeros_like(grads_ref)
    grads_ref[0:10, 0:H] = d_in[0:10]
    grads_ref[0:10, H : 2 * H] = d_in[10:20]
    grads_ref[0:10, 2 * H : 3 * H] = d_out[0:10]
    grads_ref[0:10, 3 * H : 4 * H] = d_out[10:20]
    grads_ref[10:11, 0:20] = d_b


def unpack_kernel(grads_ref, win_ref, bin_ref, woutt_ref, bout_ref):
    g = grads_ref[...]
    win_ref[0:10, :] = g[0:10, 0:H]
    win_ref[10:Q, :] = g[0:9, H : 2 * H]
    bin_ref[...] = g[9:10, H : 2 * H]
    woutt_ref[0:10, :] = g[0:10, 2 * H : 3 * H]
    woutt_ref[10:Q, :] = g[0:9, 3 * H : 4 * H]
    bout_ref[...] = g[10:11, 0:Q]


VMEM = pl.BlockSpec(memory_space=pltpu.VMEM)
SMEM = pl.BlockSpec(memory_space=pltpu.SMEM)


def shape(*dims, kind=F32):
    return jax.ShapeDtypeStruct(dims, kind)


HBM = pl.BlockSpec(memory_space=pltpu.HBM)


def prep(packed):
    return pl.pallas_call(
        prep_kernel,
        out_shape=(
            shape(HS, 3 * QS, kind=BF16),
            shape(QS, 3 * HS, kind=BF16),
            shape(QS, NZ),
        ),
        in_specs=[VMEM],
        out_specs=(VMEM,) * 3,
        compiler_params=pltpu.CompilerParams(vmem_limit_bytes=24 * MIB),
        name="prep",
    )(packed)


def middle(c1, packed, target):
    return pl.pallas_call(
        middle_kernel,
        out_shape=(
            shape(QS, 3 * HS, kind=BF16),
            shape(HS, 3 * QS, kind=BF16),
            shape(2, 16, NZ),
        ),
        in_specs=[pl.BlockSpec(memory_space=pl.ANY)] + [VMEM] * 2,
        out_specs=(VMEM,) * 3,
        compiler_params=pltpu.CompilerParams(vmem_limit_bytes=24 * MIB),
        name="middle",
    )(c1, packed, target)


def edges(populations):
    return pl.pallas_call(
        edges_kernel,
        out_shape=(shape(Q, 4, NZ), shape(Q, 4, NZ), shape(Q, 2, 16, NZ)),
        in_specs=[HBM],
        out_specs=(VMEM,) * 3,
        scratch_shapes=[pltpu.SemaphoreType.DMA],
        compiler_params=pltpu.CompilerParams(vmem_limit_bytes=24 * MIB),
        name="edges",
    )(populations)


def unpack(grads):
    win, bin_, woutt, bout = pl.pallas_call(
        unpack_kernel,
        out_shape=(shape(Q, H), shape(1, H), shape(Q, H), shape(1, Q)),
        in_specs=[VMEM],
        out_specs=(VMEM,) * 4,
        name="unpack",
    )(grads)
    return win, bin_.reshape(H), woutt.T, bout.reshape(Q)


def first(parity, bias_out, populations, before, after, lin, lout):
    return pl.pallas_call(
        first_kernel,
        out_shape=(
            shape(MSG, NZ),
            shape(MSG, NZ),
            shape(Q, 2 * W1, NZ),
            shape(G1, 2 * QS, NZ, kind=BF16),
            shape(G1, 2 * HS, NZ, kind=BF16),
        ),
        in_specs=[SMEM] + [VMEM] * 6,
        out_specs=(VMEM,) * 5,
        scratch_shapes=[pltpu.VMEM((Q, 2 * W1, NZ), F32)],
        compiler_params=pltpu.CompilerParams(vmem_limit_bytes=24 * MIB),
        name="first",
    )(parity, bias_out, populations, before, after, lin, lout)


def second(parity, bias_out, c1, msg_a, msg_b, target, lin, lout):
    return pl.pallas_call(
        second_kernel,
        out_shape=(
            shape(4, 2, 16, NZ),
            shape(32, NZ),
            shape(PG[1] - PG[0], 2 * QS, NZ, kind=BF16),
            shape(G2, 2 * HS, NZ, kind=BF16),
            shape(G2, 3, SP, NZ),
        ),
        in_specs=[SMEM] + [VMEM] * 7,
        out_specs=(VMEM,) * 5,
        scratch_shapes=[
            pltpu.VMEM((Q, 4 * W2, NZ), F32),
            pltpu.VMEM((Q, 4 * W2, NZ), F32),
        ],
        compiler_params=pltpu.CompilerParams(vmem_limit_bytes=24 * MIB),
        name="second",
    )(parity, bias_out, c1, msg_a, msg_b, target, lin, lout)


def third(parity, r, r_b, r_a, x1, h1, x2, h2, m2, lint, loutt):
    return pl.pallas_call(
        third_kernel,
        out_shape=shape(16, 128),
        in_specs=[SMEM] + [VMEM] * 10,
        out_specs=VMEM,
        scratch_shapes=[
            pltpu.VMEM((3, 2 * MARGIN + 6 * W2 + 4, NZ), F32),
            pltpu.VMEM((Q, 2 * MARGIN + 4 * W1, NZ), F32),
            pltpu.VMEM((QS, HS), F32),
            pltpu.VMEM((QS, HS), F32),
            pltpu.VMEM((QS, NZ), F32),
        ],
        compiler_params=pltpu.CompilerParams(vmem_limit_bytes=24 * MIB),
        name="third",
    )(parity, r, r_b, r_a, x1, h1, x2, h2, m2, lint, loutt)


def gather_sum(x, axes):
    peers = lax.axis_size(axes)
    copies = jnp.broadcast_to(x[None], (peers,) + x.shape)
    return jnp.sum(lax.all_to_all(copies, axes, 0, 0, tiled=True), axis=0)


def body(populations, target_density, weight_in, bias_in, weight_out, bias_out):
    gx, gy = ("zh", "zl", "x", "yh"), ("yl", "c")
    nx, ny = lax.axis_size(gx), lax.axis_size(gy)
    last, start, pops = edges(populations)
    packed = jnp.concatenate(
        [
            weight_in,
            bias_in.reshape(1, H),
            weight_out.T,
            jnp.pad(bias_out, (0, H - Q)).reshape(1, H),
        ],
        axis=0,
    )
    lin, lout, bout = prep(packed)
    before = lax.ppermute(last, gy, [(j, (j + 1) % ny) for j in range(ny)])
    after = lax.ppermute(start, gy, [((j + 1) % ny, j) for j in range(ny)])
    pair = [(i, i ^ 1) for i in range(nx)]
    cross = [(i, (i + 1) % nx if i % 2 else (i - 1) % nx) for i in range(nx)]
    parity = (lax.axis_index("yh") % 2).astype(jnp.int32).reshape(1)
    msg_a, msg_b, c1, x1, h1 = first(parity, bout, pops, before, after, lin, lout)
    lint, loutt, target = middle(c1, packed, target_density)
    got_a = lax.ppermute(msg_a, gx, pair)
    got_b = lax.ppermute(msg_b, gx, cross)
    moments, r, x2, h2, m2 = second(
        parity, bout, c1, got_a, got_b, target, lin, lout
    )
    r_a = lax.ppermute(r, gx, pair)
    r_b = lax.ppermute(r, gx, cross)
    grads = third(parity, r, r_b, r_a, x1, h1, x2, h2, m2, lint, loutt)
    grads = gather_sum(grads, ("yh", "yl", "c"))
    grads = gather_sum(grads, ("zl", "x"))
    grads = lax.psum(grads, "zh")
    return (moments, *unpack(grads))


def solution(mesh):
    fine = Mesh(mesh.devices.reshape(4, 4, 4, 2, 2, 2), ("zh", "zl", "x", "yh", "yl", "c"))
    gx, gy = ("zh", "zl", "x", "yh"), ("yl", "c")
    placed = (P(None, gx, gy, None), P(gx, gy, None), P(), P(), P(), P())
    return jax.shard_map(
        body,
        mesh=fine,
        in_specs=placed,
        out_specs=(P(None, gx, gy, None), P(), P(), P(), P()),
        check_vma=False,
    )
```

```python
import math

import jax
import jax.numpy as jnp
from jax import lax
from jax.experimental import pallas as pl
from jax.experimental.pallas import tpu as pltpu
from jax.sharding import Mesh, PartitionSpec as P

velocity_table = (
    (0, 0, 0),
    (1, 0, 0),
    (-1, 0, 0),
    (0, 1, 0),
    (0, -1, 0),
    (0, 0, 1),
    (0, 0, -1),
    (1, 1, 0),
    (-1, -1, 0),
    (1, -1, 0),
    (-1, 1, 0),
    (1, 0, 1),
    (-1, 0, -1),
    (1, 0, -1),
    (-1, 0, 1),
    (0, 1, 1),
    (0, -1, -1),
    (0, 1, -1),
    (0, -1, 1),
)
lattice_weights = (1.0 / 3.0,) + (1.0 / 18.0,) * 6 + (1.0 / 36.0,) * 12
input_scale = 8.0
output_scale = 0.05
relax_time = 0.8

Q = 19
H = 32
NZ = 256
W1 = 20
W2 = 18
G1 = 2 * W1 // 8
G2 = 4 * W2 // 8
PG = (2, 7)
MARGIN = 8
SP = 8
QS = 20 * SP
HS = H * SP
MSG = 344
F32 = jnp.float32
BF16 = jnp.bfloat16
MIB = 1024 * 1024
B1, B2, B4, B5 = 5, 9, 3, 3

to_right = [(q, -1) for q in range(19) if velocity_table[q][0] >= 0]
to_right += [(q, 0) for q in range(19) if velocity_table[q][0] == 1]
to_left = [(q, 2) for q in range(19) if velocity_table[q][0] <= 0]
to_left += [(q, 1) for q in range(19) if velocity_table[q][0] == -1]


def split(x):
    hi = x.astype(BF16)
    lo = (x - hi.astype(F32)).astype(BF16)
    return hi, lo


def mm(a, b):
    return lax.dot_general(a, b, (((1,), (0,)), ((), ())), preferred_element_type=F32)


def mm_nt(a, b):
    return lax.dot_general(a, b, (((1,), (1,)), ((), ())), preferred_element_type=F32)


def expanded(packed_ref):
    hp = lax.Precision.HIGHEST
    nn = (((1,), (0,)), ((), ()))
    eq = (
        lax.broadcasted_iota(jnp.int32, (QS, 20), 0) // SP
        == lax.broadcasted_iota(jnp.int32, (QS, 20), 1)
    ).astype(F32)
    eh = (
        lax.broadcasted_iota(jnp.int32, (HS, H), 0) // SP
        == lax.broadcasted_iota(jnp.int32, (HS, H), 1)
    ).astype(F32)
    row = lax.broadcasted_iota(jnp.int32, (20, H), 0)
    w_in = packed_ref[0:20, :] * jnp.where(row < Q, input_scale, 1.0)
    w_out = jnp.where(row < Q, packed_ref[20:40, :] * output_scale, 0.0)
    t_in = lax.dot_general(eq, w_in, nn, precision=hp, preferred_element_type=F32)
    t_out = lax.dot_general(eq, w_out, nn, precision=hp, preferred_element_type=F32)
    return eh, t_in, t_out


def put(ref, a, b):
    hp = lax.Precision.HIGHEST
    nt = (((1,), (1,)), ((), ()))
    full = lax.dot_general(a, b, nt, precision=hp, preferred_element_type=F32)
    m, n = full.shape
    row = lax.broadcasted_iota(jnp.int32, (m, n), 0)
    column = lax.broadcasted_iota(jnp.int32, (m, n), 1)
    hi, lo = split(jnp.where((row % SP) == (column % SP), full, 0.0))
    ref[:, 0:n] = hi
    ref[:, n : 2 * n] = hi
    ref[:, 2 * n : 3 * n] = lo


def prep_kernel(packed_ref, lin_ref, lout_ref, bout_ref):
    eh, t_in, t_out = expanded(packed_ref)
    put(lin_ref, eh, t_in)
    put(lout_ref, t_out, eh)
    pick = (
        lax.broadcasted_iota(jnp.int32, (QS, H), 0) // SP
        == lax.broadcasted_iota(jnp.int32, (QS, H), 1)
    ).astype(F32)
    bias = jnp.sum(pick * (packed_ref[39:40, :] * output_scale), axis=1, keepdims=True)
    bout_ref[...] = jnp.broadcast_to(bias, (QS, NZ))


def middle_kernel(after_first, packed_ref, target_in, lint_ref, loutt_ref, target_ref):
    target_ref[...] = target_in[...]
    eh, t_in, t_out = expanded(packed_ref)
    is_bias = lax.broadcasted_iota(jnp.int32, (QS, H), 0) >= Q * SP
    put(lint_ref, jnp.where(is_bias, 0.0, t_in), eh)
    put(loutt_ref, eh, t_out)


def equilibrium_parts(f):
    density = f[0]
    for q in range(1, Q):
        density = density + f[q]
    momentum = []
    for a in range(3):
        plus = None
        minus = None
        for q in range(Q):
            c = velocity_table[q][a]
            if c == 1:
                plus = f[q] if plus is None else plus + f[q]
            elif c == -1:
                minus = f[q] if minus is None else minus + f[q]
        momentum.append(plus - minus)
    return density, momentum


def project(q, m):
    out = None
    for a in range(3):
        c = velocity_table[q][a]
        if c == 0:
            continue
        if out is None:
            out = m[a] if c == 1 else -m[a]
        else:
            out = out + m[a] if c == 1 else out - m[a]
    return out


def excess_of(f):
    density, m = equilibrium_parts(f)
    base = density - 1.5 * (m[0] * m[0] + m[1] * m[1] + m[2] * m[2])
    excess = [f[0] - lattice_weights[0] * base]
    for q in range(1, Q, 2):
        w = lattice_weights[q]
        cm = project(q, m)
        even = w * (base + 4.5 * (cm * cm))
        odd = (3.0 * w) * cm
        excess.append(f[q] - (even + odd))
        excess.append(f[q + 1] - (even - odd))
    return excess, m


def rows8(x, q):
    return x[q * SP : (q + 1) * SP, :]


def batches(groups, size):
    return [range(g, min(g + size, groups)) for g in range(0, groups, size)]


def lanes(parts):
    return parts[0] if len(parts) == 1 else jnp.concatenate(parts, axis=1)


def block(x, i):
    return x[:, i * NZ : (i + 1) * NZ]


def stack3(hi, lo):
    return jnp.concatenate([hi, lo, hi], axis=0)


def collide(fs, lin_ref, lout_ref, bout_ref, save_x, save_h):
    excesses, ms, his, los = [], [], [], []
    for i, f in enumerate(fs):
        excess, m = excess_of(f)
        x = jnp.concatenate(excess + [jnp.ones((SP, NZ), F32)], axis=0)
        xhi, xlo = split(x)
        save_x(i, xhi, xlo)
        excesses.append(excess)
        ms.append(m)
        his.append(xhi)
        los.append(xlo)
    pre = mm(lin_ref[...], stack3(lanes(his), lanes(los)))
    hhi, hlo = split(jnp.tanh(pre))
    for i in range(len(fs)):
        save_h(i, block(hhi, i), block(hlo, i))
    corr = mm(lout_ref[...], stack3(hhi, hlo))
    outs = []
    for i, f in enumerate(fs):
        out = []
        for q in range(Q):
            bias = bout_ref[q * SP : (q + 1) * SP, :]
            add = block(rows8(corr, q), i) + bias
            out.append(f[q] - excesses[i][q] * (1.0 / relax_time) + add)
        outs.append(out)
    return outs, ms


def zroll(x, step):
    if step == 0:
        return x
    return pltpu.roll(x, step % NZ, 1)


def edges_kernel(pop_hbm, near_ref, far_ref, pop_ref, sem):
    copy = pltpu.make_async_copy(pop_hbm, pop_ref, sem)
    copy.start()
    copy.wait()
    odd = lax.axis_index("c") == 1
    for x in range(2):
        last = pop_ref[:, x, 14:16, :]
        start = pop_ref[:, x, 0:2, :]
        near_ref[:, 2 * x : 2 * x + 2, :] = jnp.where(odd, start, last)
        far_ref[:, 2 * x : 2 * x + 2, :] = jnp.where(odd, last, start)


def first_kernel(
    bout_ref,
    pop_ref,
    far_ref,
    near_ref,
    lin_ref,
    lout_ref,
    msg_a_ref,
    msg_b_ref,
    c1_ref,
    x1_ref,
    h1_ref,
    fs,
):
    odd = lax.axis_index("c") == 1
    for x in range(2):
        near = near_ref[:, 2 * x : 2 * x + 2, :]
        far = far_ref[:, 2 * x : 2 * x + 2, :]
        fs[:, W1 * x : W1 * x + 2, :] = jnp.where(odd, near, far)
        fs[:, W1 * x + 2 : W1 * x + 18, :] = pop_ref[:, x]
        fs[:, W1 * x + 18 : W1 * x + 20, :] = jnp.where(odd, far, near)
    for batch in batches(G1, B1):
        f = [[fs[q, 8 * g : 8 * g + 8, :] for q in range(Q)] for g in batch]

        def save_x(i, hi, lo):
            x1_ref[batch[i], 0:QS, :] = hi
            x1_ref[batch[i], QS : 2 * QS, :] = lo

        def save_h(i, hi, lo):
            h1_ref[batch[i], 0:HS, :] = hi
            h1_ref[batch[i], HS : 2 * HS, :] = lo

        outs, _m = collide(f, lin_ref, lout_ref, bout_ref, save_x, save_h)
        for g, out in zip(batch, outs):
            for q in range(Q):
                c1_ref[q, 8 * g : 8 * g + 8, :] = zroll(out[q], velocity_table[q][2])
    odd = lax.axis_index("yh") == 1

    def piece(q, plane):
        start = W1 * (plane - velocity_table[q][0]) + 1 - velocity_table[q][1]
        return c1_ref[q, start : start + W2, :]

    for k in range(Q):
        q, plane = to_right[k]
        right = piece(q, plane + 2)
        q, plane = to_left[k]
        left = piece(q, plane - 2)
        msg_a_ref[W2 * k : W2 * k + W2, :] = jnp.where(odd, left, right)
        msg_b_ref[W2 * k : W2 * k + W2, :] = jnp.where(odd, right, left)
    msg_a_ref[W2 * Q :, :] = jnp.zeros((MSG - W2 * Q, NZ), F32)
    msg_b_ref[W2 * Q :, :] = jnp.zeros((MSG - W2 * Q, NZ), F32)


def streamed(c2, x, half):
    f = []
    for q in range(Q):
        start = W2 * (x + 1) + 1 + 8 * half - W2 * velocity_table[q][0] - velocity_table[q][1]
        f.append(c2[q, start : start + 8, :])
    return f


def moments_kernel(c2_ref, moments_ref, done_ref):
    done_ref[...] = jnp.zeros_like(done_ref)
    for x in range(2):
        for half in range(2):
            rows = slice(8 * half, 8 * half + 8)
            density, m = equilibrium_parts(streamed(c2_ref, x, half))
            moments_ref[0, x, rows, :] = density
            for a in range(3):
                moments_ref[a + 1, x, rows, :] = m[a]


def second_kernel(
    bout_ref,
    c1_ref,
    msg_a_ref,
    msg_b_ref,
    target_ref,
    lin_ref,
    lout_ref,
    r_ref,
    c2,
    x2_ref,
    h2_ref,
    m2_ref,
    a1,
):
    odd = lax.axis_index("yh") == 1
    for k in range(Q):
        rows = slice(W2 * k, W2 * k + W2)
        msg_a = msg_a_ref[rows, :]
        msg_b = msg_b_ref[rows, :]
        q, plane = to_right[k]
        a1[q, W2 * (plane + 1) : W2 * (plane + 2), :] = jnp.where(odd, msg_a, msg_b)
        q, plane = to_left[k]
        a1[q, W2 * (plane + 1) : W2 * (plane + 2), :] = jnp.where(odd, msg_b, msg_a)
    for q in range(Q):
        for plane in range(-1, 3):
            source = plane - velocity_table[q][0]
            if source in (0, 1):
                start = W1 * source + 1 - velocity_table[q][1]
                a1[q, W2 * (plane + 1) : W2 * (plane + 2), :] = c1_ref[q, start : start + W2, :]
    for batch in batches(G2, B2):
        f = [[a1[q, 8 * g : 8 * g + 8, :] for q in range(Q)] for g in batch]

        def save_x(i, hi, lo):
            if PG[0] <= batch[i] < PG[1]:
                x2_ref[batch[i] - PG[0], 0:QS, :] = hi
                x2_ref[batch[i] - PG[0], QS : 2 * QS, :] = lo

        def save_h(i, hi, lo):
            h2_ref[batch[i], 0:HS, :] = hi
            h2_ref[batch[i], HS : 2 * HS, :] = lo

        outs, ms = collide(f, lin_ref, lout_ref, bout_ref, save_x, save_h)
        for g, out, m in zip(batch, outs, ms):
            for a in range(3):
                m2_ref[g, a] = m[a]
            for q in range(Q):
                c2[q, 8 * g : 8 * g + 8, :] = zroll(out[q], velocity_table[q][2])
    residual_scale = 1.0 / math.sqrt(256 * 64 * 256)
    for x in range(2):
        for half in range(2):
            f = streamed(c2, x, half)
            density = f[0]
            for q in range(1, Q):
                density = density + f[q]
            r = (density - target_ref[x, 8 * half : 8 * half + 8, :]) * residual_scale
            r_ref[16 * x + 8 * half : 16 * x + 8 * half + 8, :] = r


def third_kernel(
    _after_moments,
    r_ref,
    r_b_ref,
    r_a_ref,
    x1_ref,
    h1_ref,
    x2_ref,
    h2_ref,
    m2_ref,
    lint_ref,
    loutt_ref,
    grads_ref,
    rs,
    g1s,
    acc_in,
    acc_out,
    acc_b,
):
    odd = lax.axis_index("yh") == 1
    rs[...] = jnp.zeros_like(rs)
    g1s[...] = jnp.zeros_like(g1s)
    acc_in[...] = jnp.zeros_like(acc_in)
    acc_out[...] = jnp.zeros_like(acc_out)
    acc_b[...] = jnp.zeros_like(acc_b)
    r_a, r_b = r_a_ref[...], r_b_ref[...]
    parts = (jnp.where(odd, r_a, r_b), r_ref[...], jnp.where(odd, r_b, r_a))
    for i in range(6):
        first = MARGIN + W2 * i + 1
        for half in range(2):
            at = 16 * (i % 2) + 8 * half
            r = parts[i // 2][at : at + 8, :]
            rows = slice(first + 8 * half, first + 8 * half + 8)
            rs[0, rows, :] = r
            rs[1, rows, :] = zroll(r, -1)
            rs[2, rows, :] = zroll(r, 1)

    def hidden_pull(gqs, h_ref, batch):
        gs, ghi, glo = [], [], []
        for gq in gqs:
            g = jnp.concatenate(gq + [jnp.zeros((SP, NZ), F32)], axis=0)
            hi, lo = split(g)
            gs.append(g)
            ghi.append(hi)
            glo.append(lo)
        dh = mm(loutt_ref[...], stack3(lanes(ghi), lanes(glo)))
        dpre = []
        for i, g in enumerate(batch):
            hid = h_ref[g, 0:HS, :].astype(F32) + h_ref[g, HS : 2 * HS, :].astype(F32)
            dpre.append(block(dh, i) * (1.0 - hid * hid))
        return gs, dpre

    def add_params(gs, dpre, x_ref, h_ref, x_at, h_at):
        ghi, glo = zip(*[split(g) for g in gs])
        dhi, dlo = zip(*[split(d) for d in dpre])
        xhi = [x_ref[g, 0:QS, :] for g in x_at]
        xlo = [x_ref[g, QS : 2 * QS, :] for g in x_at]
        hhi = [h_ref[g, 0:HS, :] for g in h_at]
        hlo = [h_ref[g, HS : 2 * HS, :] for g in h_at]
        xh, xl, dh, dl = lanes(xhi), lanes(xlo), lanes(dhi), lanes(dlo)
        both = mm_nt(jnp.concatenate([xh, xl], axis=0), dh)
        acc_in[...] += both[0:QS] + both[QS:] + mm_nt(xh, dl)
        gh, gl, hh, hl = lanes(ghi), lanes(glo), lanes(hhi), lanes(hlo)
        both = mm_nt(jnp.concatenate([gh, gl], axis=0), hh)
        acc_out[...] += both[0:QS] + both[QS:] + mm_nt(gh, hl)
        acc_b[...] += sum(gs[1:], gs[0])

    def keep(x, lo, hi):
        if lo == 0 and hi == SP:
            return x
        row = lax.broadcasted_iota(jnp.int32, x.shape, 0) % SP
        return jnp.where((row >= lo) & (row < hi), x, 0.0)

    for batch in batches(G2, B4):
        gqs = []
        for g in batch:
            gq = []
            for q in range(Q):
                cx, cy, cz = velocity_table[q]
                start = MARGIN + W2 + 8 * g + W2 * cx + cy
                gq.append(rs[{0: 0, 1: 1, -1: 2}[cz], start : start + 8, :])
            gqs.append(gq)
        gs, dpre = hidden_pull(gqs, h2_ref, batch)
        kept_g, kept_d, kept_at = [], [], []
        for i, g in enumerate(batch):
            if PG[0] <= g < PG[1]:
                lo = max(W2 - 8 * g, 0)
                hi = min(3 * W2 - 8 * g, SP)
                kept_g.append(keep(gs[i], lo, hi))
                kept_d.append(keep(dpre[i], lo, hi))
                kept_at.append(g)
        if kept_at:
            add_params(kept_g, kept_d, x2_ref, h2_ref, [g - PG[0] for g in kept_at], kept_at)
        dhi, dlo = split(lanes(dpre))
        back = mm(lint_ref[...], stack3(dhi, dlo))
        for i, g in enumerate(batch):
            m = [m2_ref[g, a] for a in range(3)]
            de = [block(rows8(back, q), i) - gqs[i][q] * (1.0 / relax_time) for q in range(Q)]
            t = [lattice_weights[q] * de[q] for q in range(Q)]
            drho = t[0]
            for q in range(1, Q):
                drho = drho + t[q]
            u = [None] * Q
            for q in range(1, Q, 2):
                cm = 9.0 * project(q, m)
                u[q] = t[q] * (3.0 + cm)
                u[q + 1] = t[q + 1] * (3.0 - cm)
            dm = []
            for a in range(3):
                plus = None
                minus = None
                for q in range(Q):
                    c = velocity_table[q][a]
                    if c == 1:
                        plus = u[q] if plus is None else plus + u[q]
                    elif c == -1:
                        minus = u[q] if minus is None else minus + u[q]
                dm.append(plus - minus - 3.0 * m[a] * drho)
            for q in range(Q):
                df = gqs[i][q] + de[q] - drho
                if q:
                    df = df - project(q, dm)
                df = zroll(df, -velocity_table[q][2])
                for plane in range(4):
                    lo = max(W2 * plane, 8 * g)
                    hi = min(W2 * plane + W2, 8 * g + 8)
                    if lo < hi:
                        at = MARGIN + 1 + 2 * plane
                        g1s[q, at + lo : at + hi, :] = df[lo - 8 * g : hi - 8 * g, :]

    for batch in batches(G1, B5):
        gqs = []
        for g in batch:
            gq = []
            for q in range(Q):
                cx, cy, _cz = velocity_table[q]
                start = MARGIN + W1 + 8 * g + W1 * cx + cy
                gq.append(g1s[q, start : start + 8, :])
            gqs.append(gq)
        gs, dpre = hidden_pull(gqs, h1_ref, batch)
        add_params(gs, dpre, x1_ref, h1_ref, batch, batch)

    hp = lax.Precision.HIGHEST
    rq = lax.broadcasted_iota(jnp.int32, (QS, HS), 0)
    rh = lax.broadcasted_iota(jnp.int32, (QS, HS), 1)
    mask = (rq % SP) == (rh % SP)
    fold = (
        lax.broadcasted_iota(jnp.int32, (HS, H), 0) // SP
        == lax.broadcasted_iota(jnp.int32, (HS, H), 1)
    ).astype(F32)

    def trace(acc):
        kept = jnp.where(mask, acc[...], 0.0).reshape(20, SP, HS).sum(axis=1)
        return lax.dot_general(
            kept, fold, (((1,), (0,)), ((), ())), precision=hp, preferred_element_type=F32
        )

    q_index = lax.broadcasted_iota(jnp.int32, (20, H), 0)
    d_in = trace(acc_in) * jnp.where(q_index < Q, input_scale, 1.0)
    d_out = trace(acc_out) * output_scale
    nt = (((1,), (1,)), ((), ()))
    b_row = lax.dot_general(
        jnp.full((1, NZ), output_scale, F32), acc_b[...], nt, precision=hp, preferred_element_type=F32
    )
    d_b = lax.dot_general(
        b_row,
        (
            lax.broadcasted_iota(jnp.int32, (QS, 20), 0) // SP
            == lax.broadcasted_iota(jnp.int32, (QS, 20), 1)
        ).astype(F32),
        (((1,), (0,)), ((), ())),
        precision=hp,
        preferred_element_type=F32,
    )
    grads_ref[...] = jnp.zeros_like(grads_ref)
    grads_ref[0:10, 0:H] = d_in[0:10]
    grads_ref[0:10, H : 2 * H] = d_in[10:20]
    grads_ref[0:10, 2 * H : 3 * H] = d_out[0:10]
    grads_ref[0:10, 3 * H : 4 * H] = d_out[10:20]
    grads_ref[10:11, 0:20] = d_b


def unpack_kernel(
    grads_ref, win_hbm, bin_hbm, woutt_hbm, bout_hbm, win_ref, bin_ref, woutt_ref, bout_ref, sems
):
    g = grads_ref[...]
    copies = []

    def send(ref, hbm):
        copies.append(pltpu.make_async_copy(ref, hbm, sems.at[len(copies)]))
        copies[-1].start()

    win_ref[0:10, :] = g[0:10, 0:H]
    win_ref[10:Q, :] = g[0:9, H : 2 * H]
    send(win_ref, win_hbm)
    woutt_ref[0:10, :] = g[0:10, 2 * H : 3 * H]
    woutt_ref[10:Q, :] = g[0:9, 3 * H : 4 * H]
    send(woutt_ref, woutt_hbm)
    bin_ref[...] = g[9:10, H : 2 * H]
    send(bin_ref, bin_hbm)
    bout_ref[...] = g[10:11, 0:Q]
    send(bout_ref, bout_hbm)
    for c in copies:
        c.wait()


VMEM = pl.BlockSpec(memory_space=pltpu.VMEM)
SMEM = pl.BlockSpec(memory_space=pltpu.SMEM)


def shape(*dims, kind=F32):
    return jax.ShapeDtypeStruct(dims, kind)


HBM = pl.BlockSpec(memory_space=pltpu.HBM)


def prep(packed):
    return pl.pallas_call(
        prep_kernel,
        out_shape=(
            shape(HS, 3 * QS, kind=BF16),
            shape(QS, 3 * HS, kind=BF16),
            shape(QS, NZ),
        ),
        in_specs=[VMEM],
        out_specs=(VMEM,) * 3,
        compiler_params=pltpu.CompilerParams(vmem_limit_bytes=24 * MIB),
        name="prep",
    )(packed)


def middle(c1, packed, target):
    return pl.pallas_call(
        middle_kernel,
        out_shape=(
            shape(QS, 3 * HS, kind=BF16),
            shape(HS, 3 * QS, kind=BF16),
            shape(2, 16, NZ),
        ),
        in_specs=[pl.BlockSpec(memory_space=pl.ANY)] + [VMEM] * 2,
        out_specs=(VMEM,) * 3,
        compiler_params=pltpu.CompilerParams(vmem_limit_bytes=24 * MIB),
        name="middle",
    )(c1, packed, target)


def edges(populations):
    return pl.pallas_call(
        edges_kernel,
        out_shape=(shape(Q, 4, NZ), shape(Q, 4, NZ), shape(Q, 2, 16, NZ)),
        in_specs=[HBM],
        out_specs=(VMEM,) * 3,
        scratch_shapes=[pltpu.SemaphoreType.DMA],
        compiler_params=pltpu.CompilerParams(vmem_limit_bytes=24 * MIB),
        name="edges",
    )(populations)


def unpack(grads):
    win, bin_, woutt, bout = pl.pallas_call(
        unpack_kernel,
        out_shape=(shape(Q, H), shape(1, H), shape(Q, H), shape(1, Q)),
        in_specs=[VMEM],
        out_specs=(HBM,) * 4,
        scratch_shapes=[
            pltpu.VMEM((Q, H), F32),
            pltpu.VMEM((1, H), F32),
            pltpu.VMEM((Q, H), F32),
            pltpu.VMEM((1, Q), F32),
            pltpu.SemaphoreType.DMA((4,)),
        ],
        name="unpack",
    )(grads)
    return win, bin_.reshape(H), woutt.T, bout.reshape(Q)


def first(bias_out, populations, far, near, lin, lout):
    return pl.pallas_call(
        first_kernel,
        out_shape=(
            shape(MSG, NZ),
            shape(MSG, NZ),
            shape(Q, 2 * W1, NZ),
            shape(G1, 2 * QS, NZ, kind=BF16),
            shape(G1, 2 * HS, NZ, kind=BF16),
        ),
        in_specs=[VMEM] * 6,
        out_specs=(VMEM,) * 5,
        scratch_shapes=[pltpu.VMEM((Q, 2 * W1, NZ), F32)],
        compiler_params=pltpu.CompilerParams(vmem_limit_bytes=24 * MIB),
        name="first",
    )(bias_out, populations, far, near, lin, lout)


def second(bias_out, c1, msg_a, msg_b, target, lin, lout):
    return pl.pallas_call(
        second_kernel,
        out_shape=(
            shape(32, NZ),
            shape(Q, 4 * W2, NZ),
            shape(PG[1] - PG[0], 2 * QS, NZ, kind=BF16),
            shape(G2, 2 * HS, NZ, kind=BF16),
            shape(G2, 3, SP, NZ),
        ),
        in_specs=[VMEM] * 7,
        out_specs=(VMEM,) * 5,
        scratch_shapes=[pltpu.VMEM((Q, 4 * W2, NZ), F32)],
        compiler_params=pltpu.CompilerParams(vmem_limit_bytes=24 * MIB),
        name="second",
    )(bias_out, c1, msg_a, msg_b, target, lin, lout)


def moments_of(c2):
    return pl.pallas_call(
        moments_kernel,
        out_shape=(shape(4, 2, 16, NZ), shape(8, 128)),
        in_specs=[VMEM],
        out_specs=(VMEM,) * 2,
        compiler_params=pltpu.CompilerParams(vmem_limit_bytes=8 * MIB),
        name="moments",
    )(c2)


def third(done, r, r_b, r_a, x1, h1, x2, h2, m2, lint, loutt):
    return pl.pallas_call(
        third_kernel,
        out_shape=shape(16, 128),
        in_specs=[VMEM] * 11,
        out_specs=VMEM,
        scratch_shapes=[
            pltpu.VMEM((3, 2 * MARGIN + 6 * W2 + 4, NZ), F32),
            pltpu.VMEM((Q, 2 * MARGIN + 4 * W1, NZ), F32),
            pltpu.VMEM((QS, HS), F32),
            pltpu.VMEM((QS, HS), F32),
            pltpu.VMEM((QS, NZ), F32),
        ],
        compiler_params=pltpu.CompilerParams(vmem_limit_bytes=24 * MIB),
        name="third",
    )(done, r, r_b, r_a, x1, h1, x2, h2, m2, lint, loutt)


def gather_sum(x, axes):
    peers = lax.axis_size(axes)
    copies = jnp.broadcast_to(x[None], (peers,) + x.shape)
    return jnp.sum(lax.all_to_all(copies, axes, 0, 0, tiled=True), axis=0)


def body(populations, target_density, weight_in, bias_in, weight_out, bias_out):
    gx, gy = ("zh", "zl", "x", "yh"), ("yl", "c")
    nx, ny = lax.axis_size(gx), lax.axis_size(gy)
    near, far, pops = edges(populations)
    packed = jnp.concatenate(
        [
            weight_in,
            bias_in.reshape(1, H),
            weight_out.T,
            jnp.pad(bias_out, (0, H - Q)).reshape(1, H),
        ],
        axis=0,
    )
    lin, lout, bout = prep(packed)
    got_near = lax.ppermute(near, gy, [(j, j ^ 1) for j in range(ny)])
    got_far = lax.ppermute(far, gy, [(j, (j + 1) % ny if j % 2 else (j - 1) % ny) for j in range(ny)])
    pair = [(i, i ^ 1) for i in range(nx)]
    cross = [(i, (i + 1) % nx if i % 2 else (i - 1) % nx) for i in range(nx)]
    msg_a, msg_b, c1, x1, h1 = first(bout, pops, got_far, got_near, lin, lout)
    lint, loutt, target = middle(c1, packed, target_density)
    got_a = lax.ppermute(msg_a, gx, pair)
    got_b = lax.ppermute(msg_b, gx, cross)
    r, c2, x2, h2, m2 = second(
        bout, c1, got_a, got_b, target, lin, lout
    )
    moments, done = moments_of(c2)
    r_a = lax.ppermute(r, gx, pair)
    r_b = lax.ppermute(r, gx, cross)
    grads = third(done, r, r_b, r_a, x1, h1, x2, h2, m2, lint, loutt)
    grads = gather_sum(grads, ("x", "yh", "yl", "c"))
    grads = gather_sum(grads, ("zh", "zl"))
    return (moments, *unpack(grads))


def solution(mesh):
    fine = Mesh(mesh.devices.reshape(4, 4, 4, 2, 2, 2), ("zh", "zl", "x", "yh", "yl", "c"))
    gx, gy = ("zh", "zl", "x", "yh"), ("yl", "c")
    placed = (P(None, gx, gy, None), P(gx, gy, None), P(), P(), P(), P())
    return jax.shard_map(
        body,
        mesh=fine,
        in_specs=placed,
        out_specs=(P(None, gx, gy, None), P(), P(), P(), P()),
        check_vma=False,
    )
```

```python
import math

import jax
import jax.numpy as jnp
from jax import lax
from jax.experimental import pallas as pl
from jax.experimental.pallas import tpu as pltpu
from jax.sharding import Mesh, PartitionSpec as P

velocity_table = (
    (0, 0, 0),
    (1, 0, 0),
    (-1, 0, 0),
    (0, 1, 0),
    (0, -1, 0),
    (0, 0, 1),
    (0, 0, -1),
    (1, 1, 0),
    (-1, -1, 0),
    (1, -1, 0),
    (-1, 1, 0),
    (1, 0, 1),
    (-1, 0, -1),
    (1, 0, -1),
    (-1, 0, 1),
    (0, 1, 1),
    (0, -1, -1),
    (0, 1, -1),
    (0, -1, 1),
)
lattice_weights = (1.0 / 3.0,) + (1.0 / 18.0,) * 6 + (1.0 / 36.0,) * 12
input_scale = 8.0
output_scale = 0.05
relax_time = 0.8

Q = 19
H = 32
NZ = 256
W1 = 20
W2 = 18
G1 = 2 * W1 // 8
G2 = 4 * W2 // 8
PG = (2, 7)
MARGIN = 8
SP = 8
QS = 20 * SP
HS = H * SP
MSG = 344
F32 = jnp.float32
BF16 = jnp.bfloat16
MIB = 1024 * 1024
B1, B2, B4, B5 = 5, 9, 3, 3

to_right = [(q, -1) for q in range(19) if velocity_table[q][0] >= 0]
to_right += [(q, 0) for q in range(19) if velocity_table[q][0] == 1]
to_left = [(q, 2) for q in range(19) if velocity_table[q][0] <= 0]
to_left += [(q, 1) for q in range(19) if velocity_table[q][0] == -1]


def split(x):
    hi = x.astype(BF16)
    lo = (x - hi.astype(F32)).astype(BF16)
    return hi, lo


def mm(a, b):
    return lax.dot_general(a, b, (((1,), (0,)), ((), ())), preferred_element_type=F32)


def mm_nt(a, b):
    return lax.dot_general(a, b, (((1,), (1,)), ((), ())), preferred_element_type=F32)


def expanded(packed_ref):
    hp = lax.Precision.HIGHEST
    nn = (((1,), (0,)), ((), ()))
    eq = (
        lax.broadcasted_iota(jnp.int32, (QS, 20), 0) // SP
        == lax.broadcasted_iota(jnp.int32, (QS, 20), 1)
    ).astype(F32)
    eh = (
        lax.broadcasted_iota(jnp.int32, (HS, H), 0) // SP
        == lax.broadcasted_iota(jnp.int32, (HS, H), 1)
    ).astype(F32)
    row = lax.broadcasted_iota(jnp.int32, (20, H), 0)
    w_in = packed_ref[0:20, :] * jnp.where(row < Q, input_scale, 1.0)
    w_out = jnp.where(row < Q, packed_ref[20:40, :] * output_scale, 0.0)
    t_in = lax.dot_general(eq, w_in, nn, precision=hp, preferred_element_type=F32)
    t_out = lax.dot_general(eq, w_out, nn, precision=hp, preferred_element_type=F32)
    return eh, t_in, t_out


def put(ref, a, b):
    hp = lax.Precision.HIGHEST
    nt = (((1,), (1,)), ((), ()))
    full = lax.dot_general(a, b, nt, precision=hp, preferred_element_type=F32)
    m, n = full.shape
    row = lax.broadcasted_iota(jnp.int32, (m, n), 0)
    column = lax.broadcasted_iota(jnp.int32, (m, n), 1)
    hi, lo = split(jnp.where((row % SP) == (column % SP), full, 0.0))
    ref[:, 0:n] = hi
    ref[:, n : 2 * n] = hi
    ref[:, 2 * n : 3 * n] = lo


def prep_kernel(packed_ref, lin_ref, lout_ref, bout_ref):
    eh, t_in, t_out = expanded(packed_ref)
    put(lin_ref, eh, t_in)
    put(lout_ref, t_out, eh)
    pick = (
        lax.broadcasted_iota(jnp.int32, (QS, H), 0) // SP
        == lax.broadcasted_iota(jnp.int32, (QS, H), 1)
    ).astype(F32)
    bias = jnp.sum(pick * (packed_ref[39:40, :] * output_scale), axis=1, keepdims=True)
    bout_ref[...] = jnp.broadcast_to(bias, (QS, NZ))


def middle_kernel(after_first, packed_ref, target_in, lint_ref, loutt_ref, target_ref):
    target_ref[...] = target_in[...]
    eh, t_in, t_out = expanded(packed_ref)
    is_bias = lax.broadcasted_iota(jnp.int32, (QS, H), 0) >= Q * SP
    put(lint_ref, jnp.where(is_bias, 0.0, t_in), eh)
    put(loutt_ref, eh, t_out)


def equilibrium_parts(f):
    density = f[0]
    for q in range(1, Q):
        density = density + f[q]
    momentum = []
    for a in range(3):
        plus = None
        minus = None
        for q in range(Q):
            c = velocity_table[q][a]
            if c == 1:
                plus = f[q] if plus is None else plus + f[q]
            elif c == -1:
                minus = f[q] if minus is None else minus + f[q]
        momentum.append(plus - minus)
    return density, momentum


def project(q, m):
    out = None
    for a in range(3):
        c = velocity_table[q][a]
        if c == 0:
            continue
        if out is None:
            out = m[a] if c == 1 else -m[a]
        else:
            out = out + m[a] if c == 1 else out - m[a]
    return out


def excess_of(f):
    density, m = equilibrium_parts(f)
    base = density - 1.5 * (m[0] * m[0] + m[1] * m[1] + m[2] * m[2])
    excess = [f[0] - lattice_weights[0] * base]
    for q in range(1, Q, 2):
        w = lattice_weights[q]
        cm = project(q, m)
        even = w * (base + 4.5 * (cm * cm))
        odd = (3.0 * w) * cm
        excess.append(f[q] - (even + odd))
        excess.append(f[q + 1] - (even - odd))
    return excess, m


def rows8(x, q):
    return x[q * SP : (q + 1) * SP, :]


def batches(groups, size):
    return [range(g, min(g + size, groups)) for g in range(0, groups, size)]


def lanes(parts):
    return parts[0] if len(parts) == 1 else jnp.concatenate(parts, axis=1)


def block(x, i):
    return x[:, i * NZ : (i + 1) * NZ]


def stack3(hi, lo):
    return jnp.concatenate([hi, lo, hi], axis=0)


def collide(fs, lin_ref, lout_ref, bout_ref, save_x, save_h):
    excesses, ms, his, los = [], [], [], []
    for i, f in enumerate(fs):
        excess, m = excess_of(f)
        x = jnp.concatenate(excess + [jnp.ones((SP, NZ), F32)], axis=0)
        xhi, xlo = split(x)
        save_x(i, xhi, xlo)
        excesses.append(excess)
        ms.append(m)
        his.append(xhi)
        los.append(xlo)
    pre = mm(lin_ref[...], stack3(lanes(his), lanes(los)))
    hhi, hlo = split(jnp.tanh(pre))
    for i in range(len(fs)):
        save_h(i, block(hhi, i), block(hlo, i))
    corr = mm(lout_ref[...], stack3(hhi, hlo))
    outs = []
    for i, f in enumerate(fs):
        out = []
        for q in range(Q):
            bias = bout_ref[q * SP : (q + 1) * SP, :]
            add = block(rows8(corr, q), i) + bias
            out.append(f[q] - excesses[i][q] * (1.0 / relax_time) + add)
        outs.append(out)
    return outs, ms


def zroll(x, step):
    if step == 0:
        return x
    return pltpu.roll(x, step % NZ, 1)


def edges_kernel(pop_hbm, near_ref, far_ref, pop_ref, sem):
    copy = pltpu.make_async_copy(pop_hbm, pop_ref, sem)
    copy.start()
    copy.wait()
    odd = lax.axis_index("c") == 1
    for x in range(2):
        last = pop_ref[:, x, 14:16, :]
        start = pop_ref[:, x, 0:2, :]
        near_ref[:, 2 * x : 2 * x + 2, :] = jnp.where(odd, start, last)
        far_ref[:, 2 * x : 2 * x + 2, :] = jnp.where(odd, last, start)


def first_kernel(
    bout_ref,
    pop_ref,
    far_ref,
    near_ref,
    lin_ref,
    lout_ref,
    msg_a_ref,
    msg_b_ref,
    c1_ref,
    x1_ref,
    h1_ref,
    fs,
):
    odd = lax.axis_index("c") == 1
    for x in range(2):
        near = near_ref[:, 2 * x : 2 * x + 2, :]
        far = far_ref[:, 2 * x : 2 * x + 2, :]
        fs[:, W1 * x : W1 * x + 2, :] = jnp.where(odd, near, far)
        fs[:, W1 * x + 2 : W1 * x + 18, :] = pop_ref[:, x]
        fs[:, W1 * x + 18 : W1 * x + 20, :] = jnp.where(odd, far, near)
    for batch in batches(G1, B1):
        f = [[fs[q, 8 * g : 8 * g + 8, :] for q in range(Q)] for g in batch]

        def save_x(i, hi, lo):
            x1_ref[batch[i], 0:QS, :] = hi
            x1_ref[batch[i], QS : 2 * QS, :] = lo

        def save_h(i, hi, lo):
            h1_ref[batch[i], 0:HS, :] = hi
            h1_ref[batch[i], HS : 2 * HS, :] = lo

        outs, _m = collide(f, lin_ref, lout_ref, bout_ref, save_x, save_h)
        for g, out in zip(batch, outs):
            for q in range(Q):
                c1_ref[q, 8 * g : 8 * g + 8, :] = zroll(out[q], velocity_table[q][2])
    odd = lax.axis_index("yh") == 1

    def piece(q, plane):
        start = W1 * (plane - velocity_table[q][0]) + 1 - velocity_table[q][1]
        return c1_ref[q, start : start + W2, :]

    for k in range(Q):
        q, plane = to_right[k]
        right = piece(q, plane + 2)
        q, plane = to_left[k]
        left = piece(q, plane - 2)
        msg_a_ref[W2 * k : W2 * k + W2, :] = jnp.where(odd, left, right)
        msg_b_ref[W2 * k : W2 * k + W2, :] = jnp.where(odd, right, left)
    msg_a_ref[W2 * Q :, :] = jnp.zeros((MSG - W2 * Q, NZ), F32)
    msg_b_ref[W2 * Q :, :] = jnp.zeros((MSG - W2 * Q, NZ), F32)


def streamed(c2, x, half):
    f = []
    for q in range(Q):
        start = W2 * (x + 1) + 1 + 8 * half - W2 * velocity_table[q][0] - velocity_table[q][1]
        f.append(c2[q, start : start + 8, :])
    return f


def moments_kernel(c2_ref, moments_ref, done_ref):
    done_ref[...] = jnp.zeros_like(done_ref)
    for x in range(2):
        for half in range(2):
            rows = slice(8 * half, 8 * half + 8)
            density, m = equilibrium_parts(streamed(c2_ref, x, half))
            moments_ref[0, x, rows, :] = density
            for a in range(3):
                moments_ref[a + 1, x, rows, :] = m[a]


def second_kernel(
    bout_ref,
    c1_ref,
    msg_a_ref,
    msg_b_ref,
    target_ref,
    lin_ref,
    lout_ref,
    r_ref,
    c2,
    x2_ref,
    h2_ref,
    m2_ref,
    a1,
):
    odd = lax.axis_index("yh") == 1
    for k in range(Q):
        rows = slice(W2 * k, W2 * k + W2)
        msg_a = msg_a_ref[rows, :]
        msg_b = msg_b_ref[rows, :]
        q, plane = to_right[k]
        a1[q, W2 * (plane + 1) : W2 * (plane + 2), :] = jnp.where(odd, msg_a, msg_b)
        q, plane = to_left[k]
        a1[q, W2 * (plane + 1) : W2 * (plane + 2), :] = jnp.where(odd, msg_b, msg_a)
    for q in range(Q):
        for plane in range(-1, 3):
            source = plane - velocity_table[q][0]
            if source in (0, 1):
                start = W1 * source + 1 - velocity_table[q][1]
                a1[q, W2 * (plane + 1) : W2 * (plane + 2), :] = c1_ref[q, start : start + W2, :]
    for batch in batches(G2, B2):
        f = [[a1[q, 8 * g : 8 * g + 8, :] for q in range(Q)] for g in batch]

        def save_x(i, hi, lo):
            if PG[0] <= batch[i] < PG[1]:
                x2_ref[batch[i] - PG[0], 0:QS, :] = hi
                x2_ref[batch[i] - PG[0], QS : 2 * QS, :] = lo

        def save_h(i, hi, lo):
            h2_ref[batch[i], 0:HS, :] = hi
            h2_ref[batch[i], HS : 2 * HS, :] = lo

        outs, ms = collide(f, lin_ref, lout_ref, bout_ref, save_x, save_h)
        for g, out, m in zip(batch, outs, ms):
            for a in range(3):
                m2_ref[g, a] = m[a]
            for q in range(Q):
                c2[q, 8 * g : 8 * g + 8, :] = zroll(out[q], velocity_table[q][2])
    residual_scale = 1.0 / math.sqrt(256 * 64 * 256)
    for x in range(2):
        for half in range(2):
            f = streamed(c2, x, half)
            density = f[0]
            for q in range(1, Q):
                density = density + f[q]
            r = (density - target_ref[x, 8 * half : 8 * half + 8, :]) * residual_scale
            r_ref[16 * x + 8 * half : 16 * x + 8 * half + 8, :] = r


def third_kernel(
    _after_moments,
    r_ref,
    r_a_ref,
    r_b_ref,
    x1_ref,
    h1_ref,
    x2_ref,
    h2_ref,
    m2_ref,
    lint_ref,
    loutt_ref,
    grads_ref,
    rs,
    g1s,
    acc_in,
    acc_out,
    acc_b,
):
    odd = lax.axis_index("yh") == 1
    rs[...] = jnp.zeros_like(rs)
    g1s[...] = jnp.zeros_like(g1s)
    acc_in[...] = jnp.zeros_like(acc_in)
    acc_out[...] = jnp.zeros_like(acc_out)
    acc_b[...] = jnp.zeros_like(acc_b)
    r_a, r_b = r_a_ref[...], r_b_ref[...]
    parts = (jnp.where(odd, r_a, r_b), r_ref[...], jnp.where(odd, r_b, r_a))
    for i in range(6):
        first = MARGIN + W2 * i + 1
        for half in range(2):
            at = 16 * (i % 2) + 8 * half
            r = parts[i // 2][at : at + 8, :]
            rows = slice(first + 8 * half, first + 8 * half + 8)
            rs[0, rows, :] = r
            rs[1, rows, :] = zroll(r, -1)
            rs[2, rows, :] = zroll(r, 1)

    def hidden_pull(gqs, h_ref, batch):
        gs, ghi, glo = [], [], []
        for gq in gqs:
            g = jnp.concatenate(gq + [jnp.zeros((SP, NZ), F32)], axis=0)
            hi, lo = split(g)
            gs.append(g)
            ghi.append(hi)
            glo.append(lo)
        dh = mm(loutt_ref[...], stack3(lanes(ghi), lanes(glo)))
        dpre = []
        for i, g in enumerate(batch):
            hid = h_ref[g, 0:HS, :].astype(F32) + h_ref[g, HS : 2 * HS, :].astype(F32)
            dpre.append(block(dh, i) * (1.0 - hid * hid))
        return gs, dpre

    def add_params(gs, dpre, x_ref, h_ref, x_at, h_at):
        ghi, glo = zip(*[split(g) for g in gs])
        dhi, dlo = zip(*[split(d) for d in dpre])
        xhi = [x_ref[g, 0:QS, :] for g in x_at]
        xlo = [x_ref[g, QS : 2 * QS, :] for g in x_at]
        hhi = [h_ref[g, 0:HS, :] for g in h_at]
        hlo = [h_ref[g, HS : 2 * HS, :] for g in h_at]
        xh, xl, dh, dl = lanes(xhi), lanes(xlo), lanes(dhi), lanes(dlo)
        both = mm_nt(jnp.concatenate([xh, xl], axis=0), dh)
        acc_in[...] += both[0:QS] + both[QS:] + mm_nt(xh, dl)
        gh, gl, hh, hl = lanes(ghi), lanes(glo), lanes(hhi), lanes(hlo)
        both = mm_nt(jnp.concatenate([gh, gl], axis=0), hh)
        acc_out[...] += both[0:QS] + both[QS:] + mm_nt(gh, hl)
        acc_b[...] += sum(gs[1:], gs[0])

    def keep(x, lo, hi):
        if lo == 0 and hi == SP:
            return x
        row = lax.broadcasted_iota(jnp.int32, x.shape, 0) % SP
        return jnp.where((row >= lo) & (row < hi), x, 0.0)

    for batch in batches(G2, B4):
        gqs = []
        for g in batch:
            gq = []
            for q in range(Q):
                cx, cy, cz = velocity_table[q]
                start = MARGIN + W2 + 8 * g + W2 * cx + cy
                gq.append(rs[{0: 0, 1: 1, -1: 2}[cz], start : start + 8, :])
            gqs.append(gq)
        gs, dpre = hidden_pull(gqs, h2_ref, batch)
        kept_g, kept_d, kept_at = [], [], []
        for i, g in enumerate(batch):
            if PG[0] <= g < PG[1]:
                lo = max(W2 - 8 * g, 0)
                hi = min(3 * W2 - 8 * g, SP)
                kept_g.append(keep(gs[i], lo, hi))
                kept_d.append(keep(dpre[i], lo, hi))
                kept_at.append(g)
        if kept_at:
            add_params(kept_g, kept_d, x2_ref, h2_ref, [g - PG[0] for g in kept_at], kept_at)
        dhi, dlo = split(lanes(dpre))
        back = mm(lint_ref[...], stack3(dhi, dlo))
        for i, g in enumerate(batch):
            m = [m2_ref[g, a] for a in range(3)]
            de = [block(rows8(back, q), i) - gqs[i][q] * (1.0 / relax_time) for q in range(Q)]
            t = [lattice_weights[q] * de[q] for q in range(Q)]
            drho = t[0]
            for q in range(1, Q):
                drho = drho + t[q]
            u = [None] * Q
            for q in range(1, Q, 2):
                cm = 9.0 * project(q, m)
                u[q] = t[q] * (3.0 + cm)
                u[q + 1] = t[q + 1] * (3.0 - cm)
            dm = []
            for a in range(3):
                plus = None
                minus = None
                for q in range(Q):
                    c = velocity_table[q][a]
                    if c == 1:
                        plus = u[q] if plus is None else plus + u[q]
                    elif c == -1:
                        minus = u[q] if minus is None else minus + u[q]
                dm.append(plus - minus - 3.0 * m[a] * drho)
            for q in range(Q):
                df = gqs[i][q] + de[q] - drho
                if q:
                    df = df - project(q, dm)
                df = zroll(df, -velocity_table[q][2])
                for plane in range(4):
                    lo = max(W2 * plane, 8 * g)
                    hi = min(W2 * plane + W2, 8 * g + 8)
                    if lo < hi:
                        at = MARGIN + 1 + 2 * plane
                        g1s[q, at + lo : at + hi, :] = df[lo - 8 * g : hi - 8 * g, :]

    for batch in batches(G1, B5):
        gqs = []
        for g in batch:
            gq = []
            for q in range(Q):
                cx, cy, _cz = velocity_table[q]
                start = MARGIN + W1 + 8 * g + W1 * cx + cy
                gq.append(g1s[q, start : start + 8, :])
            gqs.append(gq)
        gs, dpre = hidden_pull(gqs, h1_ref, batch)
        add_params(gs, dpre, x1_ref, h1_ref, batch, batch)

    hp = lax.Precision.HIGHEST
    rq = lax.broadcasted_iota(jnp.int32, (QS, HS), 0)
    rh = lax.broadcasted_iota(jnp.int32, (QS, HS), 1)
    mask = (rq % SP) == (rh % SP)
    fold = (
        lax.broadcasted_iota(jnp.int32, (HS, H), 0) // SP
        == lax.broadcasted_iota(jnp.int32, (HS, H), 1)
    ).astype(F32)

    def trace(acc):
        kept = jnp.where(mask, acc[...], 0.0).reshape(20, SP, HS).sum(axis=1)
        return lax.dot_general(
            kept, fold, (((1,), (0,)), ((), ())), precision=hp, preferred_element_type=F32
        )

    q_index = lax.broadcasted_iota(jnp.int32, (20, H), 0)
    d_in = trace(acc_in) * jnp.where(q_index < Q, input_scale, 1.0)
    d_out = trace(acc_out) * output_scale
    nt = (((1,), (1,)), ((), ()))
    b_row = lax.dot_general(
        jnp.full((1, NZ), output_scale, F32), acc_b[...], nt, precision=hp, preferred_element_type=F32
    )
    d_b = lax.dot_general(
        b_row,
        (
            lax.broadcasted_iota(jnp.int32, (QS, 20), 0) // SP
            == lax.broadcasted_iota(jnp.int32, (QS, 20), 1)
        ).astype(F32),
        (((1,), (0,)), ((), ())),
        precision=hp,
        preferred_element_type=F32,
    )
    grads_ref[...] = jnp.zeros_like(grads_ref)
    grads_ref[0:10, 0:H] = d_in[0:10]
    grads_ref[0:10, H : 2 * H] = d_in[10:20]
    grads_ref[0:10, 2 * H : 3 * H] = d_out[0:10]
    grads_ref[0:10, 3 * H : 4 * H] = d_out[10:20]
    grads_ref[10:11, 0:20] = d_b


def unpack_kernel(
    grads_ref, win_hbm, bin_hbm, woutt_hbm, bout_hbm, win_ref, bin_ref, woutt_ref, bout_ref, sems
):
    g = grads_ref[...]
    copies = []

    def send(ref, hbm):
        copies.append(pltpu.make_async_copy(ref, hbm, sems.at[len(copies)]))
        copies[-1].start()

    win_ref[0:10, :] = g[0:10, 0:H]
    win_ref[10:Q, :] = g[0:9, H : 2 * H]
    send(win_ref, win_hbm)
    woutt_ref[0:10, :] = g[0:10, 2 * H : 3 * H]
    woutt_ref[10:Q, :] = g[0:9, 3 * H : 4 * H]
    send(woutt_ref, woutt_hbm)
    bin_ref[...] = g[9:10, H : 2 * H]
    send(bin_ref, bin_hbm)
    bout_ref[...] = g[10:11, 0:Q]
    send(bout_ref, bout_hbm)
    for c in copies:
        c.wait()


VMEM = pl.BlockSpec(memory_space=pltpu.VMEM)
SMEM = pl.BlockSpec(memory_space=pltpu.SMEM)


def shape(*dims, kind=F32):
    return jax.ShapeDtypeStruct(dims, kind)


HBM = pl.BlockSpec(memory_space=pltpu.HBM)


def prep(packed):
    return pl.pallas_call(
        prep_kernel,
        out_shape=(
            shape(HS, 3 * QS, kind=BF16),
            shape(QS, 3 * HS, kind=BF16),
            shape(QS, NZ),
        ),
        in_specs=[VMEM],
        out_specs=(VMEM,) * 3,
        compiler_params=pltpu.CompilerParams(vmem_limit_bytes=24 * MIB),
        name="prep",
    )(packed)


def middle(c1, packed, target):
    return pl.pallas_call(
        middle_kernel,
        out_shape=(
            shape(QS, 3 * HS, kind=BF16),
            shape(HS, 3 * QS, kind=BF16),
            shape(2, 16, NZ),
        ),
        in_specs=[pl.BlockSpec(memory_space=pl.ANY)] + [VMEM] * 2,
        out_specs=(VMEM,) * 3,
        compiler_params=pltpu.CompilerParams(vmem_limit_bytes=24 * MIB),
        name="middle",
    )(c1, packed, target)


def edges(populations):
    return pl.pallas_call(
        edges_kernel,
        out_shape=(shape(Q, 4, NZ), shape(Q, 4, NZ), shape(Q, 2, 16, NZ)),
        in_specs=[HBM],
        out_specs=(VMEM,) * 3,
        scratch_shapes=[pltpu.SemaphoreType.DMA],
        compiler_params=pltpu.CompilerParams(vmem_limit_bytes=24 * MIB),
        name="edges",
    )(populations)


def unpack(grads):
    win, bin_, woutt, bout = pl.pallas_call(
        unpack_kernel,
        out_shape=(shape(Q, H), shape(1, H), shape(Q, H), shape(1, Q)),
        in_specs=[VMEM],
        out_specs=(HBM,) * 4,
        scratch_shapes=[
            pltpu.VMEM((Q, H), F32),
            pltpu.VMEM((1, H), F32),
            pltpu.VMEM((Q, H), F32),
            pltpu.VMEM((1, Q), F32),
            pltpu.SemaphoreType.DMA((4,)),
        ],
        name="unpack",
    )(grads)
    return win, bin_.reshape(H), woutt.T, bout.reshape(Q)


def first(bias_out, populations, far, near, lin, lout):
    return pl.pallas_call(
        first_kernel,
        out_shape=(
            shape(MSG, NZ),
            shape(MSG, NZ),
            shape(Q, 2 * W1, NZ),
            shape(G1, 2 * QS, NZ, kind=BF16),
            shape(G1, 2 * HS, NZ, kind=BF16),
        ),
        in_specs=[VMEM] * 6,
        out_specs=(VMEM,) * 5,
        scratch_shapes=[pltpu.VMEM((Q, 2 * W1, NZ), F32)],
        compiler_params=pltpu.CompilerParams(vmem_limit_bytes=24 * MIB),
        name="first",
    )(bias_out, populations, far, near, lin, lout)


def second(bias_out, c1, msg_a, msg_b, target, lin, lout):
    return pl.pallas_call(
        second_kernel,
        out_shape=(
            shape(32, NZ),
            shape(Q, 4 * W2, NZ),
            shape(PG[1] - PG[0], 2 * QS, NZ, kind=BF16),
            shape(G2, 2 * HS, NZ, kind=BF16),
            shape(G2, 3, SP, NZ),
        ),
        in_specs=[VMEM] * 7,
        out_specs=(VMEM,) * 5,
        scratch_shapes=[pltpu.VMEM((Q, 4 * W2, NZ), F32)],
        compiler_params=pltpu.CompilerParams(vmem_limit_bytes=24 * MIB),
        name="second",
    )(bias_out, c1, msg_a, msg_b, target, lin, lout)


def moments_of(c2):
    return pl.pallas_call(
        moments_kernel,
        out_shape=(shape(4, 2, 16, NZ), shape(8, 128)),
        in_specs=[VMEM],
        out_specs=(VMEM,) * 2,
        compiler_params=pltpu.CompilerParams(vmem_limit_bytes=8 * MIB),
        name="moments",
    )(c2)


def third(done, r, r_a, r_b, x1, h1, x2, h2, m2, lint, loutt):
    return pl.pallas_call(
        third_kernel,
        out_shape=shape(16, 128),
        in_specs=[VMEM] * 11,
        out_specs=VMEM,
        scratch_shapes=[
            pltpu.VMEM((3, 2 * MARGIN + 6 * W2 + 4, NZ), F32),
            pltpu.VMEM((Q, 2 * MARGIN + 4 * W1, NZ), F32),
            pltpu.VMEM((QS, HS), F32),
            pltpu.VMEM((QS, HS), F32),
            pltpu.VMEM((QS, NZ), F32),
        ],
        compiler_params=pltpu.CompilerParams(vmem_limit_bytes=24 * MIB),
        name="third",
    )(done, r, r_a, r_b, x1, h1, x2, h2, m2, lint, loutt)


def gather_sum(x, axes):
    peers = lax.axis_size(axes)
    copies = jnp.broadcast_to(x[None], (peers,) + x.shape)
    return jnp.sum(lax.all_to_all(copies, axes, 0, 0, tiled=True), axis=0)


def body(populations, target_density, weight_in, bias_in, weight_out, bias_out):
    gx, gy = ("zh", "zl", "x", "yh"), ("yl", "c")
    nx, ny = lax.axis_size(gx), lax.axis_size(gy)
    near, far, pops = edges(populations)
    packed = jnp.concatenate(
        [
            weight_in,
            bias_in.reshape(1, H),
            weight_out.T,
            jnp.pad(bias_out.reshape(1, Q), ((0, 0), (0, H - Q))),
        ],
        axis=0,
    )
    lin, lout, bout = prep(packed)
    got_near = lax.ppermute(near, gy, [(j, j ^ 1) for j in range(ny)])
    got_far = lax.ppermute(far, gy, [(j, (j + 1) % ny if j % 2 else (j - 1) % ny) for j in range(ny)])
    pair = [(i, i ^ 1) for i in range(nx)]
    cross = [(i, (i + 1) % nx if i % 2 else (i - 1) % nx) for i in range(nx)]
    msg_a, msg_b, c1, x1, h1 = first(bout, pops, got_far, got_near, lin, lout)
    lint, loutt, target = middle(c1, packed, target_density)
    got_a = lax.ppermute(msg_a, gx, pair)
    got_b = lax.ppermute(msg_b, gx, cross)
    r, c2, x2, h2, m2 = second(
        bout, c1, got_a, got_b, target, lin, lout
    )
    moments, done = moments_of(c2)
    r_a = lax.ppermute(r, gx, pair)
    r_b = lax.ppermute(r, gx, cross)
    grads = third(done, r, r_a, r_b, x1, h1, x2, h2, m2, lint, loutt)
    grads = gather_sum(grads, ("x", "yh", "yl", "c"))
    grads = gather_sum(grads, ("zh", "zl"))
    return (moments, *unpack(grads))


def solution(mesh):
    fine = Mesh(mesh.devices.reshape(4, 4, 4, 2, 2, 2), ("zh", "zl", "x", "yh", "yl", "c"))
    gx, gy = ("zh", "zl", "x", "yh"), ("yl", "c")
    placed = (P(None, gx, gy, None), P(gx, gy, None), P(), P(), P(), P())
    return jax.shard_map(
        body,
        mesh=fine,
        in_specs=placed,
        out_specs=(P(None, gx, gy, None), P(), P(), P(), P()),
        check_vma=False,
    )
```

```python
import math

import jax
import jax.numpy as jnp
from jax import lax
from jax.experimental import pallas as pl
from jax.experimental.pallas import tpu as pltpu
from jax.sharding import Mesh, PartitionSpec as P

velocity_table = (
    (0, 0, 0),
    (1, 0, 0),
    (-1, 0, 0),
    (0, 1, 0),
    (0, -1, 0),
    (0, 0, 1),
    (0, 0, -1),
    (1, 1, 0),
    (-1, -1, 0),
    (1, -1, 0),
    (-1, 1, 0),
    (1, 0, 1),
    (-1, 0, -1),
    (1, 0, -1),
    (-1, 0, 1),
    (0, 1, 1),
    (0, -1, -1),
    (0, 1, -1),
    (0, -1, 1),
)
lattice_weights = (1.0 / 3.0,) + (1.0 / 18.0,) * 6 + (1.0 / 36.0,) * 12
input_scale = 8.0
output_scale = 0.05
relax_time = 0.8

Q = 19
H = 32
NZ = 256
W1 = 20
W2 = 18
G1 = 2 * W1 // 8
G2 = 4 * W2 // 8
PG = (2, 7)
MARGIN = 8
SP = 8
QS = 20 * SP
HS = H * SP
MSG = 344
F32 = jnp.float32
BF16 = jnp.bfloat16
MIB = 1024 * 1024
B1, B2, B4, B5 = 5, 9, 3, 3

to_right = [(q, -1) for q in range(19) if velocity_table[q][0] >= 0]
to_right += [(q, 0) for q in range(19) if velocity_table[q][0] == 1]
to_left = [(q, 2) for q in range(19) if velocity_table[q][0] <= 0]
to_left += [(q, 1) for q in range(19) if velocity_table[q][0] == -1]


def split(x):
    hi = x.astype(BF16)
    lo = (x - hi.astype(F32)).astype(BF16)
    return hi, lo


def mm(a, b):
    return lax.dot_general(a, b, (((1,), (0,)), ((), ())), preferred_element_type=F32)


def mm_nt(a, b):
    return lax.dot_general(a, b, (((1,), (1,)), ((), ())), preferred_element_type=F32)


def expanded(packed_ref):
    hp = lax.Precision.HIGHEST
    nn = (((1,), (0,)), ((), ()))
    eq = (
        lax.broadcasted_iota(jnp.int32, (QS, 20), 0) // SP
        == lax.broadcasted_iota(jnp.int32, (QS, 20), 1)
    ).astype(F32)
    eh = (
        lax.broadcasted_iota(jnp.int32, (HS, H), 0) // SP
        == lax.broadcasted_iota(jnp.int32, (HS, H), 1)
    ).astype(F32)
    row = lax.broadcasted_iota(jnp.int32, (20, H), 0)
    w_in = packed_ref[0:20, :] * jnp.where(row < Q, input_scale, 1.0)
    w_out = jnp.where(row < Q, packed_ref[20:40, :] * output_scale, 0.0)
    t_in = lax.dot_general(eq, w_in, nn, precision=hp, preferred_element_type=F32)
    t_out = lax.dot_general(eq, w_out, nn, precision=hp, preferred_element_type=F32)
    return eh, t_in, t_out


def put(ref, a, b):
    hp = lax.Precision.HIGHEST
    nt = (((1,), (1,)), ((), ()))
    full = lax.dot_general(a, b, nt, precision=hp, preferred_element_type=F32)
    m, n = full.shape
    row = lax.broadcasted_iota(jnp.int32, (m, n), 0)
    column = lax.broadcasted_iota(jnp.int32, (m, n), 1)
    hi, lo = split(jnp.where((row % SP) == (column % SP), full, 0.0))
    ref[:, 0:n] = hi
    ref[:, n : 2 * n] = hi
    ref[:, 2 * n : 3 * n] = lo


def prep_kernel(packed_ref, lin_ref, lout_ref, bout_ref):
    eh, t_in, t_out = expanded(packed_ref)
    put(lin_ref, eh, t_in)
    put(lout_ref, t_out, eh)
    pick = (
        lax.broadcasted_iota(jnp.int32, (QS, H), 0) // SP
        == lax.broadcasted_iota(jnp.int32, (QS, H), 1)
    ).astype(F32)
    bias = jnp.sum(pick * (packed_ref[39:40, :] * output_scale), axis=1, keepdims=True)
    bout_ref[...] = jnp.broadcast_to(bias, (QS, NZ))


def middle_kernel(after_first, packed_ref, target_in, lint_ref, loutt_ref, target_ref):
    target_ref[...] = target_in[...]
    eh, t_in, t_out = expanded(packed_ref)
    is_bias = lax.broadcasted_iota(jnp.int32, (QS, H), 0) >= Q * SP
    put(lint_ref, jnp.where(is_bias, 0.0, t_in), eh)
    put(loutt_ref, eh, t_out)


def equilibrium_parts(f):
    density = f[0]
    for q in range(1, Q):
        density = density + f[q]
    momentum = []
    for a in range(3):
        plus = None
        minus = None
        for q in range(Q):
            c = velocity_table[q][a]
            if c == 1:
                plus = f[q] if plus is None else plus + f[q]
            elif c == -1:
                minus = f[q] if minus is None else minus + f[q]
        momentum.append(plus - minus)
    return density, momentum


def project(q, m):
    out = None
    for a in range(3):
        c = velocity_table[q][a]
        if c == 0:
            continue
        if out is None:
            out = m[a] if c == 1 else -m[a]
        else:
            out = out + m[a] if c == 1 else out - m[a]
    return out


def excess_of(f):
    density, m = equilibrium_parts(f)
    base = density - 1.5 * (m[0] * m[0] + m[1] * m[1] + m[2] * m[2])
    excess = [f[0] - lattice_weights[0] * base]
    for q in range(1, Q, 2):
        w = lattice_weights[q]
        cm = project(q, m)
        even = w * (base + 4.5 * (cm * cm))
        odd = (3.0 * w) * cm
        excess.append(f[q] - (even + odd))
        excess.append(f[q + 1] - (even - odd))
    return excess, m


def rows8(x, q):
    return x[q * SP : (q + 1) * SP, :]


def batches(groups, size):
    return [range(g, min(g + size, groups)) for g in range(0, groups, size)]


def lanes(parts):
    return parts[0] if len(parts) == 1 else jnp.concatenate(parts, axis=1)


def block(x, i):
    return x[:, i * NZ : (i + 1) * NZ]


def stack3(hi, lo):
    return jnp.concatenate([hi, lo, hi], axis=0)


def collide(fs, lin_ref, lout_ref, bout_ref, save_x, save_h):
    excesses, ms, his, los = [], [], [], []
    for i, f in enumerate(fs):
        excess, m = excess_of(f)
        x = jnp.concatenate(excess + [jnp.ones((SP, NZ), F32)], axis=0)
        xhi, xlo = split(x)
        save_x(i, xhi, xlo)
        excesses.append(excess)
        ms.append(m)
        his.append(xhi)
        los.append(xlo)
    pre = mm(lin_ref[...], stack3(lanes(his), lanes(los)))
    hhi, hlo = split(jnp.tanh(pre))
    for i in range(len(fs)):
        save_h(i, block(hhi, i), block(hlo, i))
    corr = mm(lout_ref[...], stack3(hhi, hlo))
    outs = []
    for i, f in enumerate(fs):
        out = []
        for q in range(Q):
            bias = bout_ref[q * SP : (q + 1) * SP, :]
            add = block(rows8(corr, q), i) + bias
            out.append(f[q] - excesses[i][q] * (1.0 / relax_time) + add)
        outs.append(out)
    return outs, ms


def zroll(x, step):
    if step == 0:
        return x
    return pltpu.roll(x, step % NZ, 1)


def edges_kernel(pop_hbm, near_ref, far_ref, pop_ref, sem):
    copy = pltpu.make_async_copy(pop_hbm, pop_ref, sem)
    copy.start()
    copy.wait()
    odd = lax.axis_index("c") == 1
    for x in range(2):
        last = pop_ref[:, x, 14:16, :]
        start = pop_ref[:, x, 0:2, :]
        near_ref[:, 2 * x : 2 * x + 2, :] = jnp.where(odd, start, last)
        far_ref[:, 2 * x : 2 * x + 2, :] = jnp.where(odd, last, start)


def first_kernel(
    bout_ref,
    pop_ref,
    far_ref,
    near_ref,
    lin_ref,
    lout_ref,
    msg_a_ref,
    msg_b_ref,
    c1_ref,
    x1_ref,
    h1_ref,
    fs,
):
    odd = lax.axis_index("c") == 1
    for x in range(2):
        near = near_ref[:, 2 * x : 2 * x + 2, :]
        far = far_ref[:, 2 * x : 2 * x + 2, :]
        fs[:, W1 * x : W1 * x + 2, :] = jnp.where(odd, near, far)
        fs[:, W1 * x + 2 : W1 * x + 18, :] = pop_ref[:, x]
        fs[:, W1 * x + 18 : W1 * x + 20, :] = jnp.where(odd, far, near)
    for batch in batches(G1, B1):
        f = [[fs[q, 8 * g : 8 * g + 8, :] for q in range(Q)] for g in batch]

        def save_x(i, hi, lo):
            x1_ref[batch[i], 0:QS, :] = hi
            x1_ref[batch[i], QS : 2 * QS, :] = lo

        def save_h(i, hi, lo):
            h1_ref[batch[i], 0:HS, :] = hi
            h1_ref[batch[i], HS : 2 * HS, :] = lo

        outs, _m = collide(f, lin_ref, lout_ref, bout_ref, save_x, save_h)
        for g, out in zip(batch, outs):
            for q in range(Q):
                c1_ref[q, 8 * g : 8 * g + 8, :] = zroll(out[q], velocity_table[q][2])
    odd = lax.axis_index("yh") == 1

    def piece(q, plane):
        start = W1 * (plane - velocity_table[q][0]) + 1 - velocity_table[q][1]
        return c1_ref[q, start : start + W2, :]

    for k in range(Q):
        q, plane = to_right[k]
        right = piece(q, plane + 2)
        q, plane = to_left[k]
        left = piece(q, plane - 2)
        msg_a_ref[W2 * k : W2 * k + W2, :] = jnp.where(odd, left, right)
        msg_b_ref[W2 * k : W2 * k + W2, :] = jnp.where(odd, right, left)
    msg_a_ref[W2 * Q :, :] = jnp.zeros((MSG - W2 * Q, NZ), F32)
    msg_b_ref[W2 * Q :, :] = jnp.zeros((MSG - W2 * Q, NZ), F32)


def streamed(c2, x, half):
    f = []
    for q in range(Q):
        start = W2 * (x + 1) + 1 + 8 * half - W2 * velocity_table[q][0] - velocity_table[q][1]
        f.append(c2[q, start : start + 8, :])
    return f


def moments_kernel(c2_ref, moments_ref, done_ref):
    done_ref[...] = jnp.zeros_like(done_ref)
    for x in range(2):
        for half in range(2):
            rows = slice(8 * half, 8 * half + 8)
            density, m = equilibrium_parts(streamed(c2_ref, x, half))
            moments_ref[0, x, rows, :] = density
            for a in range(3):
                moments_ref[a + 1, x, rows, :] = m[a]


def second_kernel(
    bout_ref,
    c1_ref,
    msg_a_ref,
    msg_b_ref,
    target_ref,
    lin_ref,
    lout_ref,
    r_ref,
    c2,
    x2_ref,
    h2_ref,
    m2_ref,
    a1,
):
    odd = lax.axis_index("yh") == 1
    for k in range(Q):
        rows = slice(W2 * k, W2 * k + W2)
        msg_a = msg_a_ref[rows, :]
        msg_b = msg_b_ref[rows, :]
        q, plane = to_right[k]
        a1[q, W2 * (plane + 1) : W2 * (plane + 2), :] = jnp.where(odd, msg_a, msg_b)
        q, plane = to_left[k]
        a1[q, W2 * (plane + 1) : W2 * (plane + 2), :] = jnp.where(odd, msg_b, msg_a)
    for q in range(Q):
        for plane in range(-1, 3):
            source = plane - velocity_table[q][0]
            if source in (0, 1):
                start = W1 * source + 1 - velocity_table[q][1]
                a1[q, W2 * (plane + 1) : W2 * (plane + 2), :] = c1_ref[q, start : start + W2, :]
    for batch in batches(G2, B2):
        f = [[a1[q, 8 * g : 8 * g + 8, :] for q in range(Q)] for g in batch]

        def save_x(i, hi, lo):
            if PG[0] <= batch[i] < PG[1]:
                x2_ref[batch[i] - PG[0], 0:QS, :] = hi
                x2_ref[batch[i] - PG[0], QS : 2 * QS, :] = lo

        def save_h(i, hi, lo):
            h2_ref[batch[i], 0:HS, :] = hi
            h2_ref[batch[i], HS : 2 * HS, :] = lo

        outs, ms = collide(f, lin_ref, lout_ref, bout_ref, save_x, save_h)
        for g, out, m in zip(batch, outs, ms):
            for a in range(3):
                m2_ref[g, a] = m[a]
            for q in range(Q):
                c2[q, 8 * g : 8 * g + 8, :] = zroll(out[q], velocity_table[q][2])
    residual_scale = 1.0 / math.sqrt(256 * 64 * 256)
    for x in range(2):
        for half in range(2):
            f = streamed(c2, x, half)
            density = f[0]
            for q in range(1, Q):
                density = density + f[q]
            r = (density - target_ref[x, 8 * half : 8 * half + 8, :]) * residual_scale
            r_ref[16 * x + 8 * half : 16 * x + 8 * half + 8, :] = r


def third_kernel(
    _after_moments,
    r_ref,
    r_a_ref,
    r_b_ref,
    x1_ref,
    h1_ref,
    x2_ref,
    h2_ref,
    m2_ref,
    lint_ref,
    loutt_ref,
    grads_ref,
    rs,
    g1s,
    acc_in,
    acc_out,
    acc_b,
):
    odd = lax.axis_index("yh") == 1
    rs[...] = jnp.zeros_like(rs)
    g1s[...] = jnp.zeros_like(g1s)
    acc_in[...] = jnp.zeros_like(acc_in)
    acc_out[...] = jnp.zeros_like(acc_out)
    acc_b[...] = jnp.zeros_like(acc_b)
    r_a, r_b = r_a_ref[...], r_b_ref[...]
    parts = (jnp.where(odd, r_a, r_b), r_ref[...], jnp.where(odd, r_b, r_a))
    for i in range(6):
        first = MARGIN + W2 * i + 1
        for half in range(2):
            at = 16 * (i % 2) + 8 * half
            r = parts[i // 2][at : at + 8, :]
            rows = slice(first + 8 * half, first + 8 * half + 8)
            rs[0, rows, :] = r
            rs[1, rows, :] = zroll(r, -1)
            rs[2, rows, :] = zroll(r, 1)

    def hidden_pull(gqs, h_ref, batch):
        gs, ghi, glo = [], [], []
        for gq in gqs:
            g = jnp.concatenate(gq + [jnp.zeros((SP, NZ), F32)], axis=0)
            hi, lo = split(g)
            gs.append(g)
            ghi.append(hi)
            glo.append(lo)
        dh = mm(loutt_ref[...], stack3(lanes(ghi), lanes(glo)))
        dpre = []
        for i, g in enumerate(batch):
            hid = h_ref[g, 0:HS, :].astype(F32) + h_ref[g, HS : 2 * HS, :].astype(F32)
            dpre.append(block(dh, i) * (1.0 - hid * hid))
        return gs, dpre

    def add_params(gs, dpre, x_ref, h_ref, x_at, h_at):
        ghi, glo = zip(*[split(g) for g in gs])
        dhi, dlo = zip(*[split(d) for d in dpre])
        xhi = [x_ref[g, 0:QS, :] for g in x_at]
        xlo = [x_ref[g, QS : 2 * QS, :] for g in x_at]
        hhi = [h_ref[g, 0:HS, :] for g in h_at]
        hlo = [h_ref[g, HS : 2 * HS, :] for g in h_at]
        xh, xl, dh, dl = lanes(xhi), lanes(xlo), lanes(dhi), lanes(dlo)
        both = mm_nt(jnp.concatenate([xh, xl], axis=0), dh)
        acc_in[...] += both[0:QS] + both[QS:] + mm_nt(xh, dl)
        gh, gl, hh, hl = lanes(ghi), lanes(glo), lanes(hhi), lanes(hlo)
        both = mm_nt(jnp.concatenate([gh, gl], axis=0), hh)
        acc_out[...] += both[0:QS] + both[QS:] + mm_nt(gh, hl)
        acc_b[...] += sum(gs[1:], gs[0])

    def keep(x, lo, hi):
        if lo == 0 and hi == SP:
            return x
        row = lax.broadcasted_iota(jnp.int32, x.shape, 0) % SP
        return jnp.where((row >= lo) & (row < hi), x, 0.0)

    for batch in batches(G2, B4):
        gqs = []
        for g in batch:
            gq = []
            for q in range(Q):
                cx, cy, cz = velocity_table[q]
                start = MARGIN + W2 + 8 * g + W2 * cx + cy
                gq.append(rs[{0: 0, 1: 1, -1: 2}[cz], start : start + 8, :])
            gqs.append(gq)
        gs, dpre = hidden_pull(gqs, h2_ref, batch)
        kept_g, kept_d, kept_at = [], [], []
        for i, g in enumerate(batch):
            if PG[0] <= g < PG[1]:
                lo = max(W2 - 8 * g, 0)
                hi = min(3 * W2 - 8 * g, SP)
                kept_g.append(keep(gs[i], lo, hi))
                kept_d.append(keep(dpre[i], lo, hi))
                kept_at.append(g)
        if kept_at:
            add_params(kept_g, kept_d, x2_ref, h2_ref, [g - PG[0] for g in kept_at], kept_at)
        dhi, dlo = split(lanes(dpre))
        back = mm(lint_ref[...], stack3(dhi, dlo))
        for i, g in enumerate(batch):
            m = [m2_ref[g, a] for a in range(3)]
            de = [block(rows8(back, q), i) - gqs[i][q] * (1.0 / relax_time) for q in range(Q)]
            t = [lattice_weights[q] * de[q] for q in range(Q)]
            drho = t[0]
            for q in range(1, Q):
                drho = drho + t[q]
            u = [None] * Q
            for q in range(1, Q, 2):
                cm = 9.0 * project(q, m)
                u[q] = t[q] * (3.0 + cm)
                u[q + 1] = t[q + 1] * (3.0 - cm)
            dm = []
            for a in range(3):
                plus = None
                minus = None
                for q in range(Q):
                    c = velocity_table[q][a]
                    if c == 1:
                        plus = u[q] if plus is None else plus + u[q]
                    elif c == -1:
                        minus = u[q] if minus is None else minus + u[q]
                dm.append(plus - minus - 3.0 * m[a] * drho)
            for q in range(Q):
                df = gqs[i][q] + de[q] - drho
                if q:
                    df = df - project(q, dm)
                df = zroll(df, -velocity_table[q][2])
                for plane in range(4):
                    lo = max(W2 * plane, 8 * g)
                    hi = min(W2 * plane + W2, 8 * g + 8)
                    if lo < hi:
                        at = MARGIN + 1 + 2 * plane
                        g1s[q, at + lo : at + hi, :] = df[lo - 8 * g : hi - 8 * g, :]

    for batch in batches(G1, B5):
        gqs = []
        for g in batch:
            gq = []
            for q in range(Q):
                cx, cy, _cz = velocity_table[q]
                start = MARGIN + W1 + 8 * g + W1 * cx + cy
                gq.append(g1s[q, start : start + 8, :])
            gqs.append(gq)
        gs, dpre = hidden_pull(gqs, h1_ref, batch)
        add_params(gs, dpre, x1_ref, h1_ref, batch, batch)

    hp = lax.Precision.HIGHEST
    rq = lax.broadcasted_iota(jnp.int32, (QS, HS), 0)
    rh = lax.broadcasted_iota(jnp.int32, (QS, HS), 1)
    mask = (rq % SP) == (rh % SP)
    fold = (
        lax.broadcasted_iota(jnp.int32, (HS, H), 0) // SP
        == lax.broadcasted_iota(jnp.int32, (HS, H), 1)
    ).astype(F32)

    def trace(acc):
        kept = jnp.where(mask, acc[...], 0.0).reshape(20, SP, HS).sum(axis=1)
        return lax.dot_general(
            kept, fold, (((1,), (0,)), ((), ())), precision=hp, preferred_element_type=F32
        )

    q_index = lax.broadcasted_iota(jnp.int32, (20, H), 0)
    d_in = trace(acc_in) * jnp.where(q_index < Q, input_scale, 1.0)
    d_out = trace(acc_out) * output_scale
    nt = (((1,), (1,)), ((), ()))
    b_row = lax.dot_general(
        jnp.full((1, NZ), output_scale, F32), acc_b[...], nt, precision=hp, preferred_element_type=F32
    )
    d_b = lax.dot_general(
        b_row,
        (
            lax.broadcasted_iota(jnp.int32, (QS, 20), 0) // SP
            == lax.broadcasted_iota(jnp.int32, (QS, 20), 1)
        ).astype(F32),
        (((1,), (0,)), ((), ())),
        precision=hp,
        preferred_element_type=F32,
    )
    grads_ref[...] = jnp.zeros_like(grads_ref)
    grads_ref[0:10, 0:H] = d_in[0:10]
    grads_ref[0:10, H : 2 * H] = d_in[10:20]
    grads_ref[0:10, 2 * H : 3 * H] = d_out[0:10]
    grads_ref[0:10, 3 * H : 4 * H] = d_out[10:20]
    grads_ref[10:11, 0:20] = d_b


def unpack_kernel(
    grads_ref, win_hbm, bin_hbm, woutt_hbm, bout_hbm, win_ref, bin_ref, woutt_ref, bout_ref, sems
):
    g = jnp.sum(grads_ref[...], axis=0)
    copies = []

    def send(ref, hbm):
        copies.append(pltpu.make_async_copy(ref, hbm, sems.at[len(copies)]))
        copies[-1].start()

    win_ref[0:10, :] = g[0:10, 0:H]
    win_ref[10:Q, :] = g[0:9, H : 2 * H]
    send(win_ref, win_hbm)
    woutt_ref[0:10, :] = g[0:10, 2 * H : 3 * H]
    woutt_ref[10:Q, :] = g[0:9, 3 * H : 4 * H]
    send(woutt_ref, woutt_hbm)
    bin_ref[...] = g[9:10, H : 2 * H]
    send(bin_ref, bin_hbm)
    bout_ref[...] = g[10:11, 0:Q]
    send(bout_ref, bout_hbm)
    for c in copies:
        c.wait()


VMEM = pl.BlockSpec(memory_space=pltpu.VMEM)
SMEM = pl.BlockSpec(memory_space=pltpu.SMEM)


def shape(*dims, kind=F32):
    return jax.ShapeDtypeStruct(dims, kind)


HBM = pl.BlockSpec(memory_space=pltpu.HBM)


def prep(packed):
    return pl.pallas_call(
        prep_kernel,
        out_shape=(
            shape(HS, 3 * QS, kind=BF16),
            shape(QS, 3 * HS, kind=BF16),
            shape(QS, NZ),
        ),
        in_specs=[VMEM],
        out_specs=(VMEM,) * 3,
        compiler_params=pltpu.CompilerParams(vmem_limit_bytes=24 * MIB),
        name="prep",
    )(packed)


def middle(c1, packed, target):
    return pl.pallas_call(
        middle_kernel,
        out_shape=(
            shape(QS, 3 * HS, kind=BF16),
            shape(HS, 3 * QS, kind=BF16),
            shape(2, 16, NZ),
        ),
        in_specs=[pl.BlockSpec(memory_space=pl.ANY)] + [VMEM] * 2,
        out_specs=(VMEM,) * 3,
        compiler_params=pltpu.CompilerParams(vmem_limit_bytes=24 * MIB),
        name="middle",
    )(c1, packed, target)


def edges(populations):
    return pl.pallas_call(
        edges_kernel,
        out_shape=(shape(Q, 4, NZ), shape(Q, 4, NZ), shape(Q, 2, 16, NZ)),
        in_specs=[HBM],
        out_specs=(VMEM,) * 3,
        scratch_shapes=[pltpu.SemaphoreType.DMA],
        compiler_params=pltpu.CompilerParams(vmem_limit_bytes=24 * MIB),
        name="edges",
    )(populations)


def unpack(grads):
    win, bin_, woutt, bout = pl.pallas_call(
        unpack_kernel,
        out_shape=(shape(Q, H), shape(1, H), shape(Q, H), shape(1, Q)),
        in_specs=[VMEM],
        out_specs=(HBM,) * 4,
        scratch_shapes=[
            pltpu.VMEM((Q, H), F32),
            pltpu.VMEM((1, H), F32),
            pltpu.VMEM((Q, H), F32),
            pltpu.VMEM((1, Q), F32),
            pltpu.SemaphoreType.DMA((4,)),
        ],
        name="unpack",
    )(grads)
    return win, bin_.reshape(H), woutt.T, bout.reshape(Q)


def first(bias_out, populations, far, near, lin, lout):
    return pl.pallas_call(
        first_kernel,
        out_shape=(
            shape(MSG, NZ),
            shape(MSG, NZ),
            shape(Q, 2 * W1, NZ),
            shape(G1, 2 * QS, NZ, kind=BF16),
            shape(G1, 2 * HS, NZ, kind=BF16),
        ),
        in_specs=[VMEM] * 6,
        out_specs=(VMEM,) * 5,
        scratch_shapes=[pltpu.VMEM((Q, 2 * W1, NZ), F32)],
        compiler_params=pltpu.CompilerParams(vmem_limit_bytes=24 * MIB),
        name="first",
    )(bias_out, populations, far, near, lin, lout)


def second(bias_out, c1, msg_a, msg_b, target, lin, lout):
    return pl.pallas_call(
        second_kernel,
        out_shape=(
            shape(32, NZ),
            shape(Q, 4 * W2, NZ),
            shape(PG[1] - PG[0], 2 * QS, NZ, kind=BF16),
            shape(G2, 2 * HS, NZ, kind=BF16),
            shape(G2, 3, SP, NZ),
        ),
        in_specs=[VMEM] * 7,
        out_specs=(VMEM,) * 5,
        scratch_shapes=[pltpu.VMEM((Q, 4 * W2, NZ), F32)],
        compiler_params=pltpu.CompilerParams(vmem_limit_bytes=24 * MIB),
        name="second",
    )(bias_out, c1, msg_a, msg_b, target, lin, lout)


def moments_of(c2):
    return pl.pallas_call(
        moments_kernel,
        out_shape=(shape(4, 2, 16, NZ), shape(8, 128)),
        in_specs=[VMEM],
        out_specs=(VMEM,) * 2,
        compiler_params=pltpu.CompilerParams(vmem_limit_bytes=8 * MIB),
        name="moments",
    )(c2)


def third(done, r, r_a, r_b, x1, h1, x2, h2, m2, lint, loutt):
    return pl.pallas_call(
        third_kernel,
        out_shape=shape(16, 128),
        in_specs=[VMEM] * 11,
        out_specs=VMEM,
        scratch_shapes=[
            pltpu.VMEM((3, 2 * MARGIN + 6 * W2 + 4, NZ), F32),
            pltpu.VMEM((Q, 2 * MARGIN + 4 * W1, NZ), F32),
            pltpu.VMEM((QS, HS), F32),
            pltpu.VMEM((QS, HS), F32),
            pltpu.VMEM((QS, NZ), F32),
        ],
        compiler_params=pltpu.CompilerParams(vmem_limit_bytes=24 * MIB),
        name="third",
    )(done, r, r_a, r_b, x1, h1, x2, h2, m2, lint, loutt)


def gather_copies(x, axes):
    peers = lax.axis_size(axes)
    copies = jnp.broadcast_to(x[None], (peers,) + x.shape)
    return lax.all_to_all(copies, axes, 0, 0, tiled=True)


def gather_sum(x, axes):
    return jnp.sum(gather_copies(x, axes), axis=0)


def body(populations, target_density, weight_in, bias_in, weight_out, bias_out):
    gx, gy = ("zh", "zl", "x", "yh"), ("yl", "c")
    nx, ny = lax.axis_size(gx), lax.axis_size(gy)
    near, far, pops = edges(populations)
    packed = jnp.concatenate(
        [
            weight_in,
            bias_in.reshape(1, H),
            weight_out.T,
            jnp.pad(bias_out.reshape(1, Q), ((0, 0), (0, H - Q))),
        ],
        axis=0,
    )
    lin, lout, bout = prep(packed)
    got_near = lax.ppermute(near, gy, [(j, j ^ 1) for j in range(ny)])
    got_far = lax.ppermute(far, gy, [(j, (j + 1) % ny if j % 2 else (j - 1) % ny) for j in range(ny)])
    pair = [(i, i ^ 1) for i in range(nx)]
    cross = [(i, (i + 1) % nx if i % 2 else (i - 1) % nx) for i in range(nx)]
    msg_a, msg_b, c1, x1, h1 = first(bout, pops, got_far, got_near, lin, lout)
    lint, loutt, target = middle(c1, packed, target_density)
    got_a = lax.ppermute(msg_a, gx, pair)
    got_b = lax.ppermute(msg_b, gx, cross)
    r, c2, x2, h2, m2 = second(
        bout, c1, got_a, got_b, target, lin, lout
    )
    moments, done = moments_of(c2)
    r_a = lax.ppermute(r, gx, pair)
    r_b = lax.ppermute(r, gx, cross)
    grads = third(done, r, r_a, r_b, x1, h1, x2, h2, m2, lint, loutt)
    grads = gather_sum(grads, ("x", "yh", "yl", "c"))
    grads = gather_copies(grads, ("zh", "zl"))
    return (moments, *unpack(grads))


def solution(mesh):
    fine = Mesh(mesh.devices.reshape(4, 4, 4, 2, 2, 2), ("zh", "zl", "x", "yh", "yl", "c"))
    gx, gy = ("zh", "zl", "x", "yh"), ("yl", "c")
    placed = (P(None, gx, gy, None), P(gx, gy, None), P(), P(), P(), P())
    return jax.shard_map(
        body,
        mesh=fine,
        in_specs=placed,
        out_specs=(P(None, gx, gy, None), P(), P(), P(), P()),
        check_vma=False,
    )
```
